256 devices in a mesh: chan: 32 (over x_lo, z, core), stack: 8 (over x_hi, y).
Axes of the slice: x: 4 (x_hi: 2, x_lo: 2; x = x_hi * 2 + x_lo), y: 4, z: 8, core: 2. Of those that a mesh axis runs over, the one named last changes fastest.
Arguments:
- strain: bfloat16 [16, 256, 1024], P(None, 'chan', 'stack'), may hold values from -6 to 6
- sources: int32 [16, 512], P(None, 'stack'), may hold values from 0 to 255
Outputs:
- correlations: float32 [512, 256, 2048], P('stack', 'chan')
The draws below stay inside these ranges and needn't reach their ends.
All inputs are finite; a program needn't handle non-finite values.
Results may differ from the reference program's by a relative error of at most 0.0054.
Values may be sent and summed in bfloat16 or wider, within the bound.
No kernel may reach another device: no remote copies, remote signals or barrier semaphores. Data moves between devices by JAX's collectives and lax.ppermute only.
A program may use at most 64 MiB of HBM per device.

```python
import math
import jax
import jax.numpy as jnp
from jax import lax

NS = 1024
NV = 512
WINDOWS = 16
CH = 256


def plant(result, rng, low, high):
    dims = result.shape
    spot = [jax.random.randint(jax.random.fold_in(rng, axis), (), 0, dims[axis]) for axis in range(len(dims))]
    result = result.at[tuple(spot)].set(low)
    longest = dims.index(max(dims))
    spot[longest] = (spot[longest] + 1) % dims[longest]
    return result.at[tuple(spot)].set(high)


def steps_of(stream_key, shape, pieces, low, high):
    level = 1.0
    for axis_at, parts in pieces:
        draws = jax.random.uniform(jax.random.fold_in(jax.random.fold_in(stream_key, 6), axis_at), (parts,), jnp.float32, low / len(pieces), high / len(pieces))
        level = level * jnp.repeat(jnp.exp(draws), shape[axis_at] // parts).reshape((-1,) + (1,) * (len(shape) - 1 - axis_at))
    return level


def centred(stream_key, extent, scale, limit, shards=(), held_as=jnp.bfloat16):
    gain = steps_of(stream_key, extent, shards, -0.22, 0.18) if shards else 1.0
    entries = jax.random.normal(stream_key, extent, jnp.float32) * scale * gain
    return jnp.minimum(jnp.maximum(entries, -limit), limit).astype(held_as)


def setup_inputs(seed: int = 0) -> dict:
    keys = jax.random.split(jax.random.key(seed), 3)
    strain = centred(keys[0], (WINDOWS, CH, NS), 1.0, 6.0, ((1, 32), (2, 8)))
    sources = plant(jax.random.randint(keys[1], (WINDOWS, NV), 0, CH), jax.random.fold_in(keys[1], 1), 0, CH - 1).astype(jnp.int32)
    return {"strain": strain, "sources": sources}


def unpack(packed, half):
    real_part = packed[..., :half + 1]
    edge = jnp.zeros(packed.shape[:-1] + (1,), jnp.float32)
    imag_part = jnp.concatenate([edge, packed[..., half + 1:].astype(jnp.float32), edge], axis=-1)
    return (real_part.astype(jnp.float32), imag_part)

def pack(real_part, imag_part, half):
    return jnp.concatenate([real_part, imag_part[..., 1:half]], axis=-1)

def whiten(spectra, half):
    real_part, imag_part = unpack(spectra, half)
    power = real_part * real_part + imag_part * imag_part
    level = lax.optimization_barrier(jnp.mean(power, axis=-1, keepdims=True))
    factor = 1.0 / jnp.sqrt(power + 0.05 * level + 1e-06)
    return pack(real_part * factor, imag_part * factor, half)

def lag_table(half):
    width = 2 * half
    rows = jnp.arange(width, dtype=jnp.int32)[:, None]
    lags = jnp.arange(width, dtype=jnp.int32)[None, :] - half
    freq = jnp.where(rows <= half, rows, rows - half)
    phase = jnp.mod(freq * lags, width).astype(jnp.float32) * (2.0 * math.pi / width)
    weight = jnp.where((freq == 0) | (freq == half), 1.0, 2.0)
    values = jnp.where(rows <= half, weight * jnp.cos(phase), -2.0 * jnp.sin(phase))
    return (values / math.sqrt(width)).astype(jnp.bfloat16)

def stacked_cross(panel, white, half):
    panel_re, panel_im = unpack(panel.astype(jnp.float32), half)
    chan_re, chan_im = unpack(white.astype(jnp.float32), half)
    cross_re = lax.optimization_barrier(jnp.mean(panel_re[:, :, None] * chan_re[:, None] + panel_im[:, :, None] * chan_im[:, None], axis=0))
    cross_im = lax.optimization_barrier(jnp.mean(panel_re[:, :, None] * chan_im[:, None] - panel_im[:, :, None] * chan_re[:, None], axis=0))
    return pack(cross_re, cross_im, half)

def reference(strain, sources):
    half = NS
    width = 2 * NS
    transformed = jnp.fft.rfft(strain.astype(jnp.float32), n=width, axis=-1)
    spectra = jnp.concatenate([jnp.real(transformed), jnp.imag(transformed)[..., 1:half]], axis=-1).astype(jnp.float32)
    white = whiten(spectra, half).astype(jnp.bfloat16)
    panel = jax.vmap(lambda rows, picks: rows[picks])(white, sources)
    table = lag_table(half)
    block = min(64, NV)
    blocks = jnp.transpose(panel.reshape(WINDOWS, NV // block, block, width), (1, 0, 2, 3))

    def one_block(panel_block):
        cross = stacked_cross(panel_block, white, half).astype(jnp.bfloat16)
        flat = jnp.dot(cross.reshape(-1, width), table, preferred_element_type=jnp.float32)
        return flat.reshape(block, CH, width)
    return lax.map(one_block, blocks).reshape(NV, CH, width)
```

```python
import functools
import math

import jax
import jax.numpy as jnp
import ml_dtypes
import numpy as np
from jax import lax
from jax.experimental import pallas as pl
from jax.experimental.pallas import tpu as pltpu
from jax.sharding import PartitionSpec as P

NS = 1024
BF = jnp.bfloat16
F32 = jnp.float32
MESH_CORES = 2


def pair_order():
    return np.concatenate([np.arange(0, 512, 2), np.arange(1, 512, 2)])


def split_table(values):
    high = values.astype(ml_dtypes.bfloat16)
    low = (values - high.astype(np.float64)).astype(ml_dtypes.bfloat16)
    return high, low


@functools.lru_cache(None)
def forward_tables():
    freq = pair_order()
    tables = []
    for odd in range(2):
        times = np.arange(odd, NS, 2)[:, None]
        phase = (times * freq[None, :] % 2048) * (2.0 * math.pi / 2048)
        cosine, sine = np.cos(phase), np.sin(phase)
        middle = (times[:, 0] * 512 % 2048) * (2.0 * math.pi / 2048)
        sine[:, 0] = -np.sin(middle) if odd else np.cos(middle)
        tables += split_table(np.concatenate([cosine, sine], axis=1))
    return tuple(tables)


@functools.lru_cache(None)
def lag_tables():
    freq = pair_order()
    lags = np.arange(1024)[None, :]
    parts = []
    for side in (freq, 1024 - freq):
        phase = (side[:, None] * lags % 2048) * (2.0 * math.pi / 2048)
        parts.append([2.0 * np.cos(phase), -2.0 * np.sin(phase)])
    middle = (512 * lags[0] % 2048) * (2.0 * math.pi / 2048)
    parts[0][0][0] = 2.0 * np.cos(middle)
    parts[0][1][0] = -2.0 * np.sin(middle)
    parts[1][0][0] = 1.0
    parts[1][1][0] = np.where(lags[0] % 2, -1.0, 1.0)
    tables = []
    for half in range(2):
        rows = slice(256 * half, 256 * half + 256)
        stacked = np.concatenate([part[rows] for pair in parts for part in pair], axis=0)
        tables.append((stacked / math.sqrt(2048)).astype(ml_dtypes.bfloat16))
    return tuple(tables)


@functools.lru_cache(None)
def deinterleave():
    table = np.zeros((256, 256), ml_dtypes.bfloat16)
    time = np.arange(256)
    table[time, (time % 2) * 128 + time // 2] = 1
    return table


def dot(a, b, dims=((1,), (0,))):
    return lax.dot_general(a, b, (dims, ((), ())), preferred_element_type=F32)


def iota(shape, dim):
    return lax.broadcasted_iota(jnp.int32, shape, dim)


VMEM = pl.BlockSpec(memory_space=pltpu.VMEM)
SMEM = pl.BlockSpec(memory_space=pltpu.SMEM)
PARAMS = pltpu.CompilerParams(vmem_limit_bytes=44 * 1024 * 1024)


def own_kernel(place, received, perm, own, sends, even, odd):
    core, group = place[0], place[1]
    for pair in range(4):
        block = jnp.concatenate([received[2 * pair, :128], received[2 * pair + 1, :128]], axis=1)
        apart = dot(block, perm[...]).astype(BF)
        even[:, 128 * pair : 128 * pair + 128] = apart[:, :128]
        odd[:, 128 * pair : 128 * pair + 128] = apart[:, 128:]
    rows, cols = iota((128, 128), 0), iota((128, 128), 1)
    turn = rows // 8
    window = jnp.where(turn < 8, 2 * turn + core, 2 * (turn - 8) + 1 - core)
    order = (cols == window * 8 + rows % 8).astype(BF)
    own[:, :512] = dot(order, even[...]).astype(BF)
    own[:, 512:] = dot(order, odd[...]).astype(BF)
    rows, cols = iota((16, 128), 0), iota((16, 128), 1)
    for half in range(2):
        wanted = cols == (2 * group + half) * 8 + rows % 8
        pick_even = (wanted & (rows < 8)).astype(BF)
        pick_odd = (wanted & (rows >= 8)).astype(BF)
        slab = (dot(pick_even, even[...]) + dot(pick_odd, odd[...])).astype(BF)
        for other in range(16):
            sends[2 * other + half] = slab


def prepare(place, received):
    return pl.pallas_call(
        own_kernel,
        out_shape=(
            jax.ShapeDtypeStruct((128, 1024), BF),
            jax.ShapeDtypeStruct((32, 16, 512), BF),
        ),
        in_specs=[SMEM, VMEM, VMEM],
        out_specs=(VMEM, VMEM),
        scratch_shapes=[pltpu.VMEM((128, 512), BF), pltpu.VMEM((128, 512), BF)],
        compiler_params=PARAMS,
    )(place, received, jnp.asarray(deinterleave()))


def pick_kernel(place, received, window_rows, out):
    core, group = place[0], place[1]
    wanted = 2 * group + core
    picks = received[:, 128:144, :].astype(F32)
    picks = jnp.sum(jnp.where(iota(picks.shape, 1) == wanted, picks, 0.0), axis=1)
    slots = iota((512, 128), 0)
    channel = ((slots // 16) * 8 + slots % 8).astype(F32)
    lower = slots % 16 < 8
    for pair in range(4):
        both = picks[2 * pair : 2 * pair + 1] + picks[2 * pair + 1 : 2 * pair + 2]
        hit = channel == both
        for half in range(2):
            chosen = (hit & (lower if half == 0 else ~lower)).astype(F32).astype(BF)
            rows = dot(chosen, window_rows[...], ((0,), (0,)))
            out[128 * pair : 128 * pair + 128, 512 * half : 512 * half + 512] = rows.astype(BF)


def pick(place, received, window_rows):
    return pl.pallas_call(
        pick_kernel,
        out_shape=jax.ShapeDtypeStruct((512, 1024), BF),
        in_specs=[SMEM, VMEM, VMEM],
        out_specs=VMEM,
        compiler_params=PARAMS,
    )(place, received, window_rows)


def white_kernel(rows_ref, even_hi, even_lo, odd_hi, odd_lo, out, evens, odds):
    count = rows_ref.shape[0]
    even, odd = rows_ref[:, :512], rows_ref[:, 512:]
    evens[...] = dot(even, even_hi[...]) + dot(even, even_lo[...])
    odds[...] = dot(odd, odd_hi[...]) + dot(odd, odd_lo[...])

    def strip(step, carry):
        at = pl.ds(pl.multiple_of(step * 16, 16), 16)
        a, c = evens[at, :512], evens[at, 512:]
        b, d = odds[at, :512], odds[at, 512:]
        first = iota((16, 512), 1) == 0
        re_1 = jnp.where(first, c, a + b)
        im_1 = jnp.where(first, d, -c - d)
        re_2 = jnp.where(first, a + b, a - b)
        im_2 = jnp.where(first, a - b, c - d)
        power_1 = re_1 * re_1 + im_1 * im_1
        square_re, square_im = re_2 * re_2, im_2 * im_2
        power_2 = square_re + square_im
        level = jnp.sum(power_1 + power_2, axis=1, keepdims=True) * (1.0 / 1025.0)
        floor = 0.05 * level + 1e-06
        factor_1 = lax.rsqrt(power_1 + floor)
        factor_re = lax.rsqrt(jnp.where(first, square_re, power_2) + floor)
        factor_im = lax.rsqrt(jnp.where(first, square_im, power_2) + floor)
        parts = (re_1 * factor_1, im_1 * factor_1, re_2 * factor_re, im_2 * factor_im)
        for half in range(2):
            for index, part in enumerate(parts):
                start = 1024 * half + 256 * index
                out[at, start : start + 256] = part[:, 256 * half : 256 * half + 256].astype(BF)
        return carry

    lax.fori_loop(0, count // 16, strip, 0)


def whiten(rows, block):
    count = rows.shape[0]
    whole = pl.BlockSpec((512, 1024), lambda i: (0, 0))
    return pl.pallas_call(
        white_kernel,
        out_shape=jax.ShapeDtypeStruct((count, 2048), BF),
        grid=(count // block,),
        in_specs=[pl.BlockSpec((block, 1024), lambda i: (i, 0))] + [whole] * 4,
        out_specs=pl.BlockSpec((block, 2048), lambda i: (i, 0)),
        scratch_shapes=[pltpu.VMEM((block, 1024), F32), pltpu.VMEM((block, 1024), F32)],
        compiler_params=PARAMS,
    )(rows, *[jnp.asarray(t) for t in forward_tables()])


SOURCES = 16


def cross_kernel(near, far, own, lag_even, lag_odd, out, panel, mine, cross):
    @pl.when(pl.program_id(0) == 0)
    def _():
        for w in range(16):
            if w % 2 == 0:
                mine[w : w + 2] = own[8 * w : 8 * w + 16].astype(F32).reshape(2, 8, 2048)

    for w in range(8):
        for group in range(16):
            lane = slice(128 * group, 128 * group + 128)
            panel[w, group] = near[w, :, lane].astype(F32)
            panel[8 + w, group] = far[w, :, lane].astype(F32)

    def pair_of_sources(step, carry):
        for chunk in range(4):
            groups = [8 * (chunk // 2) + chunk % 2 + 2 * k for k in range(4)]
            lanes = [slice(128 * group, 128 * group + 128) for group in groups]
            sums = [[None] * 5, [None] * 5]
            for w in range(16):
                own_parts = [mine[w, :, lane] for lane in lanes]
                for which in range(2):
                    row = step * 2 + which
                    picked = [
                        panel[w, group, pl.ds(row, 8, stride=0), :] for group in groups
                    ]
                    terms = [
                        picked[0] * own_parts[0] + picked[1] * own_parts[1],
                        picked[0] * own_parts[1] - picked[1] * own_parts[0],
                        picked[2] * own_parts[2],
                        picked[3] * own_parts[3],
                        picked[2] * own_parts[3] - picked[3] * own_parts[2],
                    ]
                    if chunk:
                        terms[2:4] = [terms[2] + terms[3], None]
                    total = sums[which]
                    for k, term in enumerate(terms):
                        if term is not None:
                            total[k] = term if total[k] is None else total[k] + term
            results = []
            for re_1, im_1, re_2, edge, im_2 in sums:
                if chunk == 0:
                    first = iota((8, 128), 1) == 0
                    im_2 = jnp.where(first, edge, im_2)
                    re_2 = jnp.where(first, re_2, re_2 + edge)
                results.append((re_1, im_1, re_2, im_2))
            rows = pl.ds(pl.multiple_of(step * 16, 16), 16)
            for lane, upper, lower in zip(lanes, *results):
                both = jnp.concatenate([upper, lower], axis=0) * (1.0 / 16.0)
                cross[rows, lane] = both.astype(BF)
        return carry

    lax.fori_loop(0, SOURCES // 2, pair_of_sources, 0)
    evens = dot(cross[:, :1024], lag_even[...])
    odds = dot(cross[:, 1024:], lag_odd[...])
    out[:, :, :1024] = (evens - odds).reshape(SOURCES, 8, 1024)
    out[:, :, 1024:] = (evens + odds).reshape(SOURCES, 8, 1024)


def correlate(near, far, own):
    panel = pl.BlockSpec((8, SOURCES, 2048), lambda i: (0, i, 0))
    lag = pl.BlockSpec((1024, 1024), lambda i: (0, 0))
    return pl.pallas_call(
        cross_kernel,
        out_shape=jax.ShapeDtypeStruct((64, 8, 2048), F32),
        grid=(64 // SOURCES,),
        in_specs=[panel, panel, pl.BlockSpec((128, 2048), lambda i: (0, 0)), lag, lag],
        out_specs=pl.BlockSpec((SOURCES, 8, 2048), lambda i: (i, 0, 0)),
        scratch_shapes=[
            pltpu.VMEM((16, 16, SOURCES, 128), F32),
            pltpu.VMEM((16, 8, 2048), F32),
            pltpu.VMEM((SOURCES * 8, 2048), BF),
        ],
        compiler_params=PARAMS,
    )(near, far, own, *[jnp.asarray(t) for t in lag_tables()])


def local(strain, sources):
    chan, group = lax.axis_index("chan"), lax.axis_index("stack")
    place = jnp.stack([chan % 2, group]).astype(jnp.int32)
    picks = sources.astype(BF)
    blank = jnp.zeros_like(picks)
    side = group % 2 == 0
    picks = jnp.concatenate([jnp.where(side, picks, blank), jnp.where(side, blank, picks)], axis=1)
    block = jnp.concatenate([strain.reshape(128, 128), picks], axis=0)
    block = jnp.broadcast_to(block[None], (8, 144, 128))
    received = lax.all_to_all(block, "stack", 0, 0, tiled=True)
    own, sends = prepare(place, received)
    window_rows = lax.all_to_all(sends, "chan", 0, 0, tiled=True)
    picked = pick(place, received, window_rows.reshape(512, 512))
    near = lax.all_to_all(picked.reshape(8, 64, 1024), "stack", 0, 0, tiled=True)
    near = near.reshape(512, 1024)
    far = lax.ppermute(near, "chan", [(i, i ^ 1) for i in range(32)])
    own_white = whiten(own, 128)
    near_white = whiten(near, 512).reshape(8, 64, 2048)
    far_white = whiten(far, 512).reshape(8, 64, 2048)
    return correlate(near_white, far_white, own_white)


def solution(mesh):
    placed = (P(None, "chan", "stack"), P(None, "stack"))
    return jax.shard_map(
        local, mesh=mesh, in_specs=placed, out_specs=P("stack", "chan", None), check_vma=False
    )
```

```python
import functools
import math

import jax
import jax.numpy as jnp
import ml_dtypes
import numpy as np
from jax import lax
from jax.experimental import pallas as pl
from jax.experimental.pallas import tpu as pltpu
from jax.sharding import PartitionSpec as P

NS = 1024
BF = jnp.bfloat16
F32 = jnp.float32
MESH_CORES = 2


def pair_order():
    return np.concatenate([np.arange(0, 512, 2), np.arange(1, 512, 2)])


def split_table(values):
    high = values.astype(ml_dtypes.bfloat16)
    low = (values - high.astype(np.float64)).astype(ml_dtypes.bfloat16)
    return high, low


@functools.lru_cache(None)
def forward_tables():
    freq = pair_order()
    tables = []
    for odd in range(2):
        times = np.arange(odd, NS, 2)[:, None]
        phase = (times * freq[None, :] % 2048) * (2.0 * math.pi / 2048)
        cosine, sine = np.cos(phase), np.sin(phase)
        middle = (times[:, 0] * 512 % 2048) * (2.0 * math.pi / 2048)
        sine[:, 0] = -np.sin(middle) if odd else np.cos(middle)
        tables += split_table(np.concatenate([cosine, sine], axis=1))
    return tuple(tables)


@functools.lru_cache(None)
def lag_tables():
    freq = pair_order()
    lags = np.arange(1024)[None, :]
    parts = []
    for side in (freq, 1024 - freq):
        phase = (side[:, None] * lags % 2048) * (2.0 * math.pi / 2048)
        parts.append([2.0 * np.cos(phase), -2.0 * np.sin(phase)])
    middle = (512 * lags[0] % 2048) * (2.0 * math.pi / 2048)
    parts[0][0][0] = 2.0 * np.cos(middle)
    parts[0][1][0] = -2.0 * np.sin(middle)
    parts[1][0][0] = 1.0
    parts[1][1][0] = np.where(lags[0] % 2, -1.0, 1.0)
    tables = []
    for half in range(2):
        rows = slice(256 * half, 256 * half + 256)
        stacked = np.concatenate([part[rows] for pair in parts for part in pair], axis=0)
        tables.append((stacked / math.sqrt(2048)).astype(ml_dtypes.bfloat16))
    return tuple(tables)


@functools.lru_cache(None)
def deinterleave():
    table = np.zeros((256, 256), ml_dtypes.bfloat16)
    time = np.arange(256)
    table[time, (time % 2) * 128 + time // 2] = 1
    return table


def dot(a, b, dims=((1,), (0,))):
    return lax.dot_general(a, b, (dims, ((), ())), preferred_element_type=F32)


def iota(shape, dim):
    return lax.broadcasted_iota(jnp.int32, shape, dim)


VMEM = pl.BlockSpec(memory_space=pltpu.VMEM)
PARAMS = pltpu.CompilerParams(vmem_limit_bytes=44 * 1024 * 1024)


def place():
    return lax.axis_index("chan") % MESH_CORES, lax.axis_index("stack")


def pack_kernel(strain, sources, out):
    _, group = place()
    picks = sources[...].astype(F32)
    both = jnp.concatenate([picks, picks], axis=1)
    both = jnp.where(iota((16, 128), 1) // 64 == group % 2, both, 0.0).astype(BF)
    for other in range(8):
        out[other, :128] = strain[...]
        out[other, 128:] = both


def pack(strain, sources):
    return pl.pallas_call(
        pack_kernel,
        out_shape=jax.ShapeDtypeStruct((8, 144, 128), BF),
        in_specs=[VMEM, VMEM],
        out_specs=VMEM,
        compiler_params=PARAMS,
    )(strain, sources)


def own_kernel(received, perm, own, sends, even, odd):
    core, group = place()
    for pair in range(4):
        block = jnp.concatenate([received[2 * pair, :128], received[2 * pair + 1, :128]], axis=1)
        apart = dot(block, perm[...]).astype(BF)
        even[:, 128 * pair : 128 * pair + 128] = apart[:, :128]
        odd[:, 128 * pair : 128 * pair + 128] = apart[:, 128:]
    rows, cols = iota((16, 128), 0), iota((16, 128), 1)
    for half in range(2):
        wanted = cols == (2 * group + half) * 8 + rows % 8
        pick_even = (wanted & (rows < 8)).astype(F32).astype(BF)
        pick_odd = (wanted & (rows >= 8)).astype(F32).astype(BF)
        slab = (dot(pick_even, even[...]) + dot(pick_odd, odd[...])).astype(BF)
        for other in range(16):
            sends[2 * other + half] = slab
    rows, cols = iota((128, 128), 0), iota((128, 128), 1)
    turn = rows // 8
    window = jnp.where(turn < 8, 2 * turn + core, 2 * (turn - 8) + 1 - core)
    order = (cols == window * 8 + rows % 8).astype(F32).astype(BF)
    own[:, :512] = dot(order, even[...]).astype(BF)
    own[:, 512:] = dot(order, odd[...]).astype(BF)


def prepare(received):
    return pl.pallas_call(
        own_kernel,
        out_shape=(
            jax.ShapeDtypeStruct((128, 1024), BF),
            jax.ShapeDtypeStruct((32, 16, 512), BF),
        ),
        in_specs=[VMEM, VMEM],
        out_specs=(VMEM, VMEM),
        scratch_shapes=[pltpu.VMEM((128, 512), BF), pltpu.VMEM((128, 512), BF)],
        compiler_params=PARAMS,
    )(received, jnp.asarray(deinterleave()))


def pick_kernel(received, window_rows, out):
    core, group = place()
    wanted = 2 * group + core
    picks = received[:, 128:144, :].astype(F32)
    picks = jnp.sum(jnp.where(iota(picks.shape, 1) == wanted, picks, 0.0), axis=1)
    slots = iota((512, 128), 0)
    channel = ((slots // 16) * 8 + slots % 8).astype(F32)
    lower = slots % 16 < 8
    for pair in range(4):
        both = picks[2 * pair : 2 * pair + 1] + picks[2 * pair + 1 : 2 * pair + 2]
        hit = channel == both
        for half in range(2):
            chosen = (hit & (lower if half == 0 else ~lower)).astype(F32).astype(BF)
            rows = dot(chosen, window_rows[...], ((0,), (0,)))
            out[128 * pair : 128 * pair + 128, 512 * half : 512 * half + 512] = rows.astype(BF)


def pick(received, window_rows):
    return pl.pallas_call(
        pick_kernel,
        out_shape=jax.ShapeDtypeStruct((512, 1024), BF),
        in_specs=[VMEM, VMEM],
        out_specs=VMEM,
        compiler_params=PARAMS,
    )(received, window_rows)


def whiten_strips(count, evens, odds, store):
    def strip(step, carry):
        at = pl.ds(pl.multiple_of(step * 16, 16), 16)
        first = iota((16, 128), 1) == 0
        held, total = [], None
        for k in range(4):
            near, far = slice(128 * k, 128 * k + 128), slice(512 + 128 * k, 640 + 128 * k)
            a, c, b, d = evens[at, near], evens[at, far], odds[at, near], odds[at, far]
            re_1, im_1, re_2, im_2 = a + b, c + d, a - b, c - d
            if k == 0:
                re_2, im_2 = jnp.where(first, re_1, re_2), jnp.where(first, re_2, im_2)
                re_1, im_1 = jnp.where(first, c, re_1), jnp.where(first, -d, im_1)
            power_1 = re_1 * re_1 + im_1 * im_1
            square_re, square_im = re_2 * re_2, im_2 * im_2
            power_2 = square_re + square_im
            both = power_1 + power_2
            total = both if total is None else total + both
            held.append((re_1, im_1, re_2, im_2, power_1, square_re, square_im, power_2))
        level = jnp.sum(total, axis=1, keepdims=True) * (1.0 / 1025.0)
        floor = 0.05 * level + 1e-06
        for k, (re_1, im_1, re_2, im_2, power_1, square_re, square_im, power_2) in enumerate(held):
            factor_1 = lax.rsqrt(power_1 + floor)
            if k == 0:
                factor_re = lax.rsqrt(jnp.where(first, square_re, power_2) + floor)
                factor_im = lax.rsqrt(jnp.where(first, square_im, power_2) + floor)
            else:
                factor_re = factor_im = lax.rsqrt(power_2 + floor)
            parts = (re_1 * factor_1, -im_1 * factor_1, re_2 * factor_re, im_2 * factor_im)
            for index, part in enumerate(parts):
                store(step, 8 * (k // 2) + 2 * index + k % 2, part.astype(BF))
        return carry

    lax.fori_loop(0, count // 16, strip, 0, unroll=4)


def transform(rows, tables, evens, odds):
    even_hi, even_lo, odd_hi, odd_lo = tables
    even, odd = rows[:, :512], rows[:, 512:]
    evens[...] = dot(even, even_hi[...]) + dot(even, even_lo[...])
    odds[...] = dot(odd, odd_hi[...]) + dot(odd, odd_lo[...])


def own_white_kernel(rows, even_hi, even_lo, odd_hi, odd_lo, out, evens, odds):
    transform(rows[...], (even_hi, even_lo, odd_hi, odd_lo), evens, odds)

    def store(step, lane_group, part):
        out[pl.ds(2 * step, 2), lane_group] = part.astype(F32).reshape(2, 8, 128)

    whiten_strips(128, evens, odds, store)


def panel_white_kernel(half, rows, even_hi, even_lo, odd_hi, odd_lo, out, evens, odds):
    picked = rows[:, 32 * half : 32 * half + 32, :].reshape(256, 1024)
    transform(picked, (even_hi, even_lo, odd_hi, odd_lo), evens, odds)

    def store(step, lane_group, part):
        at = pl.ds(pl.multiple_of(step % 2 * 16, 16), 16)
        out[step // 2, at, 128 * lane_group : 128 * lane_group + 128] = part

    whiten_strips(256, evens, odds, store)


def white_call(kernel, rows, count, shape, dtype):
    return pl.pallas_call(
        kernel,
        out_shape=jax.ShapeDtypeStruct(shape, dtype),
        in_specs=[VMEM] * 5,
        out_specs=VMEM,
        scratch_shapes=[pltpu.VMEM((count, 1024), F32), pltpu.VMEM((count, 1024), F32)],
        compiler_params=PARAMS,
        cost_estimate=pl.CostEstimate(
            flops=count * 2**22, bytes_accessed=2**22 + count * 2**13, transcendentals=count * 1024
        ),
    )(rows, *[jnp.asarray(t) for t in forward_tables()])


SOURCES = 32
CHANNELS = 4
PIECES = 4


def cross_kernel(half, near, far, own, lag_even, lag_odd, *rest):
    out, raw, cross, stage, sems = rest[-5:]
    turns = 8 // CHANNELS

    def block(step, carry):
        tile, start = step // turns, step % turns * CHANNELS
        rows = pl.ds(pl.multiple_of(tile * 16, 16), 16)
        for chunk in range(4):
            groups = [8 * (chunk // 2) + chunk % 2 + 2 * k for k in range(4)]
            sums = [[None] * 5 for _ in range(2 * CHANNELS)]
            for w in range(16):
                side = near if w < 8 else far
                tall = [side[w % 8, rows, 128 * g : 128 * g + 128].astype(F32) for g in groups]
                for c in range(CHANNELS):
                    mine = [own[w, g, pl.ds(start + c, 8, stride=0), :] for g in groups]
                    for t in range(2):
                        picked = [values[8 * t : 8 * t + 8] for values in tall]
                        terms = [
                            picked[0] * mine[0] + picked[1] * mine[1],
                            picked[0] * mine[1] - picked[1] * mine[0],
                            picked[2] * mine[2],
                            picked[3] * mine[3],
                            picked[2] * mine[3] - picked[3] * mine[2],
                        ]
                        if chunk:
                            terms[2:4] = [terms[2] + terms[3], None]
                        total = sums[2 * c + t]
                        for k, term in enumerate(terms):
                            if term is not None:
                                total[k] = term if total[k] is None else total[k] + term
            for index, (re_1, im_1, re_2, edge, im_2) in enumerate(sums):
                if chunk == 0:
                    first = iota((8, 128), 1) == 0
                    im_2 = jnp.where(first, edge, im_2)
                    re_2 = jnp.where(first, re_2, re_2 + edge)
                lowest = tile * 128 + index % 2 * 64 + start + index // 2
                for g, part in zip(groups, (re_1, im_1, re_2, im_2)):
                    raw[g, pl.ds(lowest, 8, stride=8), :] = part
        return carry

    lax.fori_loop(0, SOURCES // 16 * turns, block, 0)
    for g in range(16):
        cross[:, 128 * g : 128 * g + 128] = (raw[g] * (1.0 / 16.0)).astype(BF)
    width = 1024 // PIECES
    copies = []
    for piece in range(PIECES):
        lower = slice(width * piece, width * piece + width)
        upper = slice(1024 + width * piece, 1024 + width * piece + width)
        evens = dot(cross[:, :1024], lag_even[:, lower])
        odds = dot(cross[:, 1024:], lag_odd[:, lower])
        stage[:, :, lower] = (evens - odds).reshape(SOURCES, 8, width)
        stage[:, :, upper] = (evens + odds).reshape(SOURCES, 8, width)
        for lanes in (lower, upper):
            copy = pltpu.make_async_copy(
                stage.at[:, :, lanes],
                out.at[SOURCES * half : SOURCES * half + SOURCES, :, lanes],
                sems.at[len(copies)],
            )
            copy.start()
            copies.append(copy)
    for copy in copies:
        copy.wait()


def correlate(half, near, far, own, earlier=None):
    anywhere = pl.BlockSpec(memory_space=pl.ANY)
    operands = [near, far, own, *[jnp.asarray(t) for t in lag_tables()]]
    specs = [VMEM] * 5
    aliases = {}
    if earlier is not None:
        aliases = {len(operands): 0}
        operands.append(earlier)
        specs.append(anywhere)
    return pl.pallas_call(
        functools.partial(cross_kernel, half),
        out_shape=jax.ShapeDtypeStruct((64, 8, 2048), F32),
        in_specs=specs,
        out_specs=anywhere,
        input_output_aliases=aliases,
        scratch_shapes=[
            pltpu.VMEM((16, SOURCES * 8, 128), F32),
            pltpu.VMEM((SOURCES * 8, 2048), BF),
            pltpu.VMEM((SOURCES, 8, 2048), F32),
            pltpu.SemaphoreType.DMA((2 * PIECES,)),
        ],
        compiler_params=PARAMS,
        cost_estimate=pl.CostEstimate(
            flops=3 * 2**30, bytes_accessed=9 * 2**20, transcendentals=0
        ),
    )(*operands)


def local(strain, sources):
    block = pack(strain.reshape(128, 128), sources)
    received = lax.all_to_all(block, "stack", 0, 0, tiled=True)
    own, sends = prepare(received)
    window_rows = lax.all_to_all(sends, "chan", 0, 0, tiled=True)
    own_white = white_call(own_white_kernel, own, 128, (16, 16, 8, 128), F32)
    picked = pick(received, window_rows.reshape(512, 512))
    picked, own_white = lax.optimization_barrier((picked, own_white))
    rows = lax.all_to_all(picked.reshape(8, 64, 1024), "stack", 0, 0, tiled=True)
    near, far = [], []
    for half in range(2):
        kernel = functools.partial(panel_white_kernel, half)
        near.append(white_call(kernel, rows, 256, (8, 32, 2048), BF))
        far.append(lax.ppermute(near[half], "chan", [(i, i ^ 1) for i in range(32)]))
    result = correlate(0, near[0], far[0], own_white)
    return correlate(1, near[1], far[1], own_white, result)


def solution(mesh):
    placed = (P(None, "chan", "stack"), P(None, "stack"))
    return jax.shard_map(
        local, mesh=mesh, in_specs=placed, out_specs=P("stack", "chan", None), check_vma=False
    )
```

```python
import functools
import math

import jax
import jax.numpy as jnp
import ml_dtypes
import numpy as np
from jax import lax
from jax.experimental import pallas as pl
from jax.experimental.pallas import tpu as pltpu
from jax.sharding import PartitionSpec as P

NS = 1024
BF = jnp.bfloat16
F32 = jnp.float32
MESH_CORES = 2
PIECES = 4


def pair_order():
    return np.concatenate([np.arange(0, 512, 2), np.arange(1, 512, 2)])


def split_table(values):
    high = values.astype(ml_dtypes.bfloat16)
    low = (values - high.astype(np.float64)).astype(ml_dtypes.bfloat16)
    return high, low


@functools.lru_cache(None)
def forward_tables():
    freq = pair_order()
    tables = []
    for odd in range(2):
        times = np.arange(odd, NS, 2)[:, None]
        phase = (times * freq[None, :] % 2048) * (2.0 * math.pi / 2048)
        cosine, sine = np.cos(phase), np.sin(phase)
        middle = (times[:, 0] * 512 % 2048) * (2.0 * math.pi / 2048)
        sine[:, 0] = -np.sin(middle) if odd else np.cos(middle)
        tables += split_table(np.concatenate([cosine, sine], axis=1))
    return tuple(tables)


@functools.lru_cache(None)
def lag_tables():
    freq = pair_order()
    lags = np.arange(1024)[None, :]
    parts = []
    for side in (freq, 1024 - freq):
        phase = (side[:, None] * lags % 2048) * (2.0 * math.pi / 2048)
        parts.append([2.0 * np.cos(phase), -2.0 * np.sin(phase)])
    middle = (512 * lags[0] % 2048) * (2.0 * math.pi / 2048)
    parts[0][0][0] = 2.0 * np.cos(middle)
    parts[0][1][0] = -2.0 * np.sin(middle)
    parts[1][0][0] = 1.0
    parts[1][1][0] = np.where(lags[0] % 2, -1.0, 1.0)
    tables = []
    for half in range(2):
        rows = slice(256 * half, 256 * half + 256)
        stacked = np.concatenate([part[rows] for pair in parts for part in pair], axis=0)
        tables.append((stacked / math.sqrt(2048)).astype(ml_dtypes.bfloat16))
    return tuple(tables)


@functools.lru_cache(None)
def deinterleave():
    table = np.zeros((256, 256), ml_dtypes.bfloat16)
    time = np.arange(256)
    table[time, (time % 2) * 128 + time // 2] = 1
    return table


def dot(a, b, dims=((1,), (0,))):
    return lax.dot_general(a, b, (dims, ((), ())), preferred_element_type=F32)


def iota(shape, dim):
    return lax.broadcasted_iota(jnp.int32, shape, dim)


VMEM = pl.BlockSpec(memory_space=pltpu.VMEM)
ANYWHERE = pl.BlockSpec(memory_space=pl.ANY)
PARAMS = pltpu.CompilerParams(vmem_limit_bytes=16 * 1024 * 1024)


def place():
    return lax.axis_index("chan") % MESH_CORES, lax.axis_index("stack")


def cost(flops, moved=2**20, special=0):
    return pl.CostEstimate(flops=flops, bytes_accessed=moved, transcendentals=special)


def spread_kernel(strain, sends, sems):
    copies = []
    for other in range(32):
        windows = strain.at[8 * (other % 2) : 8 * (other % 2) + 8]
        copies.append(pltpu.make_async_copy(windows, sends.at[other], sems.at[other]))
    for copy in copies:
        copy.start()
    for copy in copies:
        copy.wait()


def spread(strain):
    return pl.pallas_call(
        spread_kernel,
        out_shape=jax.ShapeDtypeStruct((32, 8, 8, 128), BF),
        in_specs=[ANYWHERE],
        out_specs=ANYWHERE,
        scratch_shapes=[pltpu.SemaphoreType.DMA((32,))],
        compiler_params=PARAMS,
        cost_estimate=cost(2**32),
    )(strain)


def share_kernel(strain, sources, shared):
    _, group = place()
    picks = sources[...].astype(F32)
    both = jnp.concatenate([picks, picks], axis=1)
    both = jnp.where(iota((16, 128), 1) // 64 == group % 2, both, 0.0)
    shared[:16] = strain[...]
    shared[16:] = both.reshape(2, 8, 128).astype(BF)


def share(strain, sources):
    return pl.pallas_call(
        share_kernel,
        out_shape=jax.ShapeDtypeStruct((18, 8, 128), BF),
        in_specs=[VMEM, VMEM],
        out_specs=VMEM,
        compiler_params=PARAMS,
        cost_estimate=cost(2**28),
    )(strain, sources)


def pick_kernel(window_rows, *rest):
    shared, (out, blocks, picks) = rest[:8], rest[-3:]
    core, group = place()
    for k in range(8):
        picks[group ^ k] = shared[k][16:].astype(F32).reshape(16, 128)
        blocks[group ^ k] = shared[k][:16]
    chosen = iota((16, 8), 0) == 8 * core + iota((16, 8), 1)
    chosen = chosen.astype(F32).astype(BF)
    columns = []
    for pair in range(4):
        both = (picks[2 * pair] + picks[2 * pair + 1]).astype(BF)
        columns.append(dot(both, chosen, ((0,), (0,))))
    column = jnp.concatenate(columns, axis=0)
    channel = iota((512, 256), 1).astype(F32)
    for w in range(8):
        hits = (column[:, w : w + 1] == channel).astype(F32).astype(BF)
        rows = window_rows[:, w].astype(F32).reshape(256, 128).astype(BF)
        found = dot(hits, rows).astype(BF)
        for other in range(8):
            out[other, 64 * w : 64 * w + 64] = found[64 * other : 64 * other + 64]


def pick(window_rows, shared):
    return pl.pallas_call(
        pick_kernel,
        out_shape=(
            jax.ShapeDtypeStruct((8, 512, 128), BF),
            jax.ShapeDtypeStruct((8, 16, 8, 128), BF),
        ),
        in_specs=[VMEM] * 9,
        out_specs=(VMEM, VMEM),
        scratch_shapes=[pltpu.VMEM((8, 16, 128), F32)],
        compiler_params=PARAMS,
        cost_estimate=cost(2**33),
    )(window_rows, *shared)


def whiten_strips(start, count, evens, odds, store):
    def strip(step, carry):
        at = pl.ds(pl.multiple_of(start + step * 16, 16), 16)
        first = iota((16, 128), 1) == 0
        held, total = [], None
        for k in range(4):
            near, far = slice(128 * k, 128 * k + 128), slice(512 + 128 * k, 640 + 128 * k)
            a, c, b, d = evens[at, near], evens[at, far], odds[at, near], odds[at, far]
            re_1, im_1, re_2, im_2 = a + b, c + d, a - b, c - d
            if k == 0:
                re_2, im_2 = jnp.where(first, re_1, re_2), jnp.where(first, re_2, im_2)
                re_1, im_1 = jnp.where(first, c, re_1), jnp.where(first, -d, im_1)
            power_1 = re_1 * re_1 + im_1 * im_1
            square_re, square_im = re_2 * re_2, im_2 * im_2
            power_2 = square_re + square_im
            both = power_1 + power_2
            total = both if total is None else total + both
            held.append((re_1, im_1, re_2, im_2, power_1, square_re, square_im, power_2))
        level = jnp.sum(total, axis=1, keepdims=True) * (1.0 / 1025.0)
        floor = 0.05 * level + 1e-06
        for k, (re_1, im_1, re_2, im_2, power_1, square_re, square_im, power_2) in enumerate(held):
            factor_1 = lax.rsqrt(power_1 + floor)
            if k == 0:
                factor_re = lax.rsqrt(jnp.where(first, square_re, power_2) + floor)
                factor_im = lax.rsqrt(jnp.where(first, square_im, power_2) + floor)
            else:
                factor_re = factor_im = lax.rsqrt(power_2 + floor)
            parts = (re_1 * factor_1, -im_1 * factor_1, re_2 * factor_re, im_2 * factor_im)
            for index, part in enumerate(parts):
                store(step, 8 * (k // 2) + 2 * index + k % 2, part.astype(BF))
        return carry

    lax.fori_loop(0, count // 16, strip, 0, unroll=4)


def transform(blocks, perm, table, evens, odds):
    even, odd = [], []
    for pair in range(4):
        block = jnp.concatenate(blocks[2 * pair : 2 * pair + 2], axis=1)
        apart = dot(block, perm[...]).astype(BF)
        even.append(apart[:, :128])
        odd.append(apart[:, 128:])
    even, odd = jnp.concatenate(even, axis=1), jnp.concatenate(odd, axis=1)
    evens[...] = dot(even, table[0][...]) + dot(even, table[1][...])
    odds[...] = dot(odd, table[2][...]) + dot(odd, table[3][...])


def panel_blocks(rows, half):
    blocks = []
    for k in range(8):
        wanted = rows[k].reshape(8, 64, 128)[:, 32 * half : 32 * half + 32]
        blocks.append(wanted.reshape(256, 128))
    return blocks


def panel_store(out, step, lane_group, part):
    at = pl.ds(pl.multiple_of(step % 2 * 16, 16), 16)
    out[step // 2, at, 128 * lane_group : 128 * lane_group + 128] = part


def first_white_kernel(perm, *refs):
    table, (rows, out, evens, odds) = refs[:4], refs[4:]
    transform(panel_blocks(rows, 0), perm, table, evens, odds)
    whiten_strips(0, 256, evens, odds, functools.partial(panel_store, out))


def second_white_kernel(perm, *refs):
    table, (rows, mine, out, own, evens, odds, held) = refs[:4], refs[4:]
    core, _ = place()
    parts = []
    for k, block in enumerate(panel_blocks(rows, 1)):
        parts.append(jnp.concatenate([block, mine[k].astype(F32).reshape(128, 128).astype(BF)]))
    transform(parts, perm, table, evens, odds)
    whiten_strips(0, 256, evens, odds, functools.partial(panel_store, out))

    def store(step, lane_group, part):
        held[lane_group, pl.ds(pl.multiple_of(step * 16, 16), 16)] = part.astype(F32)

    whiten_strips(256, 128, evens, odds, store)
    first = iota((8, 128), 1) == 0

    def arrange(step, carry):
        window = lax.rem(step + 8 * core, 16)
        at = pl.ds(pl.multiple_of(step * 8, 8), 8)
        for chunk in range(8):
            re = held[real_group(chunk), at]
            im = held[real_group(chunk) + 2, at]
            own[window, 3 * chunk] = re
            own[window, 3 * chunk + 1] = jnp.where(first, im, im - re) if chunk == 1 else im - re
            own[window, 3 * chunk + 2] = im + re
        return carry

    lax.fori_loop(0, 16, arrange, 0, unroll=2)


def real_group(chunk):
    lanes, pair = chunk // 2, chunk % 2
    return 8 * (lanes // 2) + lanes % 2 + 4 * pair


def white_call(kernel, count, shapes, operands, scratch=()):
    return pl.pallas_call(
        kernel,
        out_shape=shapes,
        in_specs=[VMEM] * len(operands),
        out_specs=[VMEM] * len(shapes),
        scratch_shapes=[pltpu.VMEM((count, 1024), F32), pltpu.VMEM((count, 1024), F32), *scratch],
        compiler_params=PARAMS,
        cost_estimate=cost(count * 2**23, 2**22 + count * 2**13, count * 1024),
    )(*operands)


SOURCES = 32
CHANNELS = 4


def cross_kernel(half, near, far, own, lag_even, lag_odd, *rest):
    out, raw, cross, stage, sems = rest[-5:]
    turns = 8 // CHANNELS

    def block(step, carry):
        tile, start = step // turns, step % turns * CHANNELS
        rows = pl.ds(pl.multiple_of(tile * 16, 16), 16)
        first = iota((16, 128), 1) == 0
        for chunk in range(8):
            group = real_group(chunk)
            sums = [[None] * 3 for _ in range(2 * CHANNELS)]
            for w in range(16):
                side = near if w < 8 else far
                re = side[w % 8, rows, 128 * group : 128 * group + 128].astype(F32)
                im = side[w % 8, rows, 128 * group + 256 : 128 * group + 384].astype(F32)
                both = re + (jnp.where(first, 0.0, im) if chunk == 1 else im)
                for c in range(CHANNELS):
                    at = pl.ds(start + c, 8, stride=0)
                    mine = [own[w, 3 * chunk + k, at, :] for k in range(3)]
                    for t in range(2):
                        total = sums[2 * c + t]
                        for k, picked in enumerate((both, im, re)):
                            term = picked[8 * t : 8 * t + 8] * mine[k]
                            total[k] = term if total[k] is None else total[k] + term
            for index, (a, b, c) in enumerate(sums):
                if chunk == 1:
                    edge = first[:8]
                    results = jnp.where(edge, a, a + b), jnp.where(edge, b, c - a)
                else:
                    results = a + b, c - a
                lowest = tile * 128 + index % 2 * 64 + start + index // 2
                for k, part in enumerate(results):
                    raw[group + 2 * k, pl.ds(lowest, 8, stride=8), :] = part
        return carry

    lax.fori_loop(0, SOURCES // 16 * turns, block, 0)
    for g in range(16):
        cross[:, 128 * g : 128 * g + 128] = (raw[g] * (1.0 / 16.0)).astype(BF)
    width = 1024 // PIECES
    copies = []
    for piece in range(PIECES):
        lower = slice(width * piece, width * piece + width)
        upper = slice(1024 + width * piece, 1024 + width * piece + width)
        evens = dot(cross[:, :1024], lag_even[:, lower])
        odds = dot(cross[:, 1024:], lag_odd[:, lower])
        stage[:, :, lower] = (evens - odds).reshape(SOURCES, 8, width)
        stage[:, :, upper] = (evens + odds).reshape(SOURCES, 8, width)
        for lanes in (lower, upper):
            copy = pltpu.make_async_copy(
                stage.at[:, :, lanes],
                out.at[SOURCES * half : SOURCES * half + SOURCES, :, lanes],
                sems.at[len(copies)],
            )
            copy.start()
            copies.append(copy)
    for copy in copies:
        copy.wait()


def correlate(half, near, far, own, lag, earlier=None):
    operands = [near, far, own, *lag]
    specs = [VMEM] * 5
    aliases = {}
    if earlier is not None:
        aliases = {len(operands): 0}
        operands.append(earlier)
        specs.append(ANYWHERE)
    return pl.pallas_call(
        functools.partial(cross_kernel, half),
        out_shape=jax.ShapeDtypeStruct((64, 8, 2048), F32),
        in_specs=specs,
        out_specs=ANYWHERE,
        input_output_aliases=aliases,
        scratch_shapes=[
            pltpu.VMEM((16, SOURCES * 8, 128), F32),
            pltpu.VMEM((SOURCES * 8, 2048), BF),
            pltpu.VMEM((SOURCES, 8, 2048), F32),
            pltpu.SemaphoreType.DMA((2 * PIECES,)),
        ],
        compiler_params=PARAMS,
        cost_estimate=pl.CostEstimate(
            flops=3 * 2**30, bytes_accessed=9 * 2**20, transcendentals=0
        ),
    )(*operands)


def local(strain, sources):
    window_rows = lax.all_to_all(spread(strain), "chan", 0, 0, tiled=True)
    shared = share(strain, sources)
    everyone = [shared]
    for k in range(1, 8):
        everyone.append(lax.ppermute(shared, "stack", [(j, j ^ k) for j in range(8)]))
    picked, blocks = pick(window_rows, everyone)
    rows = lax.all_to_all(picked, "stack", 0, 0, tiled=True)
    tables = [jnp.asarray(t) for t in (deinterleave(), *forward_tables())]
    lag = [jnp.asarray(t) for t in lag_tables()]
    panel = jax.ShapeDtypeStruct((8, 32, 2048), BF)
    mine = jax.ShapeDtypeStruct((16, 24, 8, 128), F32)
    swap = functools.partial(lax.ppermute, axis_name="chan", perm=[(i, i ^ 1) for i in range(32)])
    (near_0,) = white_call(first_white_kernel, 256, [panel], [*tables, rows])
    far_0 = swap(near_0)
    held = [pltpu.VMEM((16, 128, 128), F32)]
    near_1, own = white_call(second_white_kernel, 384, [panel, mine], [*tables, rows, blocks], held)
    far_1 = swap(near_1)
    result = correlate(0, near_0, far_0, own, lag)
    return correlate(1, near_1, far_1, own, lag, result)


def solution(mesh):
    placed = (P(None, "chan", "stack"), P(None, "stack"))
    return jax.shard_map(
        local, mesh=mesh, in_specs=placed, out_specs=P("stack", "chan", None), check_vma=False
    )
```

```python
import functools
import math

import jax
import jax.numpy as jnp
import ml_dtypes
import numpy as np
from jax import lax
from jax.experimental import pallas as pl
from jax.experimental.pallas import tpu as pltpu
from jax.sharding import PartitionSpec as P

NS = 1024
BF = jnp.bfloat16
F32 = jnp.float32
MESH_CORES = 2
PIECES = 4


def pair_order():
    return np.concatenate([np.arange(0, 512, 2), np.arange(1, 512, 2)])


def split_table(values):
    high = values.astype(ml_dtypes.bfloat16)
    low = (values - high.astype(np.float64)).astype(ml_dtypes.bfloat16)
    return high, low


@functools.lru_cache(None)
def forward_tables():
    freq = pair_order()
    tables = []
    for odd in range(2):
        times = np.arange(odd, NS, 2)[:, None]
        phase = (times * freq[None, :] % 2048) * (2.0 * math.pi / 2048)
        cosine, sine = np.cos(phase), np.sin(phase)
        middle = (times[:, 0] * 512 % 2048) * (2.0 * math.pi / 2048)
        sine[:, 0] = -np.sin(middle) if odd else np.cos(middle)
        tables += split_table(np.concatenate([cosine, sine], axis=1))
    return tuple(tables)


@functools.lru_cache(None)
def lag_tables():
    freq = pair_order()
    lags = np.arange(1024)[None, :]
    parts = []
    for side in (freq, 1024 - freq):
        phase = (side[:, None] * lags % 2048) * (2.0 * math.pi / 2048)
        parts.append([2.0 * np.cos(phase), -2.0 * np.sin(phase)])
    middle = (512 * lags[0] % 2048) * (2.0 * math.pi / 2048)
    parts[0][0][0] = 2.0 * np.cos(middle)
    parts[0][1][0] = -2.0 * np.sin(middle)
    parts[1][0][0] = 1.0
    parts[1][1][0] = np.where(lags[0] % 2, -1.0, 1.0)
    tables = []
    for half in range(2):
        rows = slice(256 * half, 256 * half + 256)
        stacked = np.concatenate([part[rows] for pair in parts for part in pair], axis=0)
        tables.append((stacked / math.sqrt(2048)).astype(ml_dtypes.bfloat16))
    return tuple(tables)


@functools.lru_cache(None)
def deinterleave():
    table = np.zeros((256, 256), ml_dtypes.bfloat16)
    time = np.arange(256)
    table[time, (time % 2) * 128 + time // 2] = 1
    return table


def dot(a, b, dims=((1,), (0,))):
    return lax.dot_general(a, b, (dims, ((), ())), preferred_element_type=F32)


def iota(shape, dim):
    return lax.broadcasted_iota(jnp.int32, shape, dim)


VMEM = pl.BlockSpec(memory_space=pltpu.VMEM)
ANYWHERE = pl.BlockSpec(memory_space=pl.ANY)
PARAMS = pltpu.CompilerParams(vmem_limit_bytes=16 * 1024 * 1024)


def place():
    return lax.axis_index("chan") % MESH_CORES, lax.axis_index("stack")


def cost(flops, moved=2**20, special=0):
    return pl.CostEstimate(flops=flops, bytes_accessed=moved, transcendentals=special)


def spread_kernel(strain, sends, sems):
    copies = []
    for other in range(32):
        windows = strain.at[8 * (other % 2) : 8 * (other % 2) + 8]
        copies.append(pltpu.make_async_copy(windows, sends.at[other], sems.at[other]))
    for copy in copies:
        copy.start()
    for copy in copies:
        copy.wait()


def spread(strain):
    return pl.pallas_call(
        spread_kernel,
        out_shape=jax.ShapeDtypeStruct((32, 8, 8, 128), BF),
        in_specs=[ANYWHERE],
        out_specs=ANYWHERE,
        scratch_shapes=[pltpu.SemaphoreType.DMA((32,))],
        compiler_params=PARAMS,
        cost_estimate=cost(2**32),
    )(strain)


def share_kernel(strain, sources, shared):
    _, group = place()
    picks = sources[...].astype(F32)
    both = jnp.concatenate([picks, picks], axis=1)
    both = jnp.where(iota((16, 128), 1) // 64 == group % 2, both, 0.0)
    shared[:16] = strain[...]
    shared[16:] = both.reshape(2, 8, 128).astype(BF)


def share(strain, sources):
    return pl.pallas_call(
        share_kernel,
        out_shape=jax.ShapeDtypeStruct((18, 8, 128), BF),
        in_specs=[VMEM, VMEM],
        out_specs=VMEM,
        compiler_params=PARAMS,
        cost_estimate=cost(2**28),
    )(strain, sources)


def pick_kernel(window_rows, *rest):
    shared, (out, blocks, picks) = rest[:8], rest[-3:]
    core, group = place()
    for k in range(8):
        sender = group ^ (k + core * (8 - 2 * k) if k else 0)
        picks[sender] = shared[k][16:].astype(F32).reshape(16, 128)
        blocks[sender] = shared[k][:16]
    chosen = iota((16, 8), 0) == 8 * core + iota((16, 8), 1)
    chosen = chosen.astype(F32).astype(BF)
    columns = []
    for pair in range(4):
        both = (picks[2 * pair] + picks[2 * pair + 1]).astype(BF)
        columns.append(dot(both, chosen, ((0,), (0,))))
    column = jnp.concatenate(columns, axis=0)
    channel = iota((512, 256), 1).astype(F32)
    for w in range(8):
        hits = (column[:, w : w + 1] == channel).astype(F32).astype(BF)
        rows = window_rows[:, w].astype(F32).reshape(256, 128).astype(BF)
        found = dot(hits, rows).astype(BF)
        for other in range(8):
            out[other, 64 * w : 64 * w + 64] = found[64 * other : 64 * other + 64]


def pick(window_rows, shared):
    return pl.pallas_call(
        pick_kernel,
        out_shape=(
            jax.ShapeDtypeStruct((8, 512, 128), BF),
            jax.ShapeDtypeStruct((8, 16, 8, 128), BF),
        ),
        in_specs=[VMEM] * 9,
        out_specs=(VMEM, VMEM),
        scratch_shapes=[pltpu.VMEM((8, 16, 128), F32)],
        compiler_params=PARAMS,
        cost_estimate=cost(2**33),
    )(window_rows, *shared)


def whiten_strips(start, count, evens, odds, store):
    def strip(step, carry):
        at = pl.ds(pl.multiple_of(start + step * 16, 16), 16)
        first = iota((16, 128), 1) == 0
        held, total = [], None
        for k in range(4):
            near, far = slice(128 * k, 128 * k + 128), slice(512 + 128 * k, 640 + 128 * k)
            a, c, b, d = evens[at, near], evens[at, far], odds[at, near], odds[at, far]
            re_1, im_1, re_2, im_2 = a + b, c + d, a - b, c - d
            if k == 0:
                re_2, im_2 = jnp.where(first, re_1, re_2), jnp.where(first, re_2, im_2)
                re_1, im_1 = jnp.where(first, c, re_1), jnp.where(first, -d, im_1)
            power_1 = re_1 * re_1 + im_1 * im_1
            square_re, square_im = re_2 * re_2, im_2 * im_2
            power_2 = square_re + square_im
            both = power_1 + power_2
            total = both if total is None else total + both
            held.append((re_1, im_1, re_2, im_2, power_1, square_re, square_im, power_2))
        level = jnp.sum(total, axis=1, keepdims=True) * (1.0 / 1025.0)
        floor = 0.05 * level + 1e-06
        for k, (re_1, im_1, re_2, im_2, power_1, square_re, square_im, power_2) in enumerate(held):
            factor_1 = lax.rsqrt(power_1 + floor)
            if k == 0:
                factor_re = lax.rsqrt(jnp.where(first, square_re, power_2) + floor)
                factor_im = lax.rsqrt(jnp.where(first, square_im, power_2) + floor)
            else:
                factor_re = factor_im = lax.rsqrt(power_2 + floor)
            parts = (re_1 * factor_1, -im_1 * factor_1, re_2 * factor_re, im_2 * factor_im)
            for index, part in enumerate(parts):
                store(step, 8 * (k // 2) + 2 * index + k % 2, part.astype(BF))
        return carry

    lax.fori_loop(0, count // 16, strip, 0, unroll=4)


def transform(blocks, perm, table, evens, odds):
    even, odd = [], []
    for pair in range(4):
        block = jnp.concatenate(blocks[2 * pair : 2 * pair + 2], axis=1)
        apart = dot(block, perm[...]).astype(BF)
        even.append(apart[:, :128])
        odd.append(apart[:, 128:])
    even, odd = jnp.concatenate(even, axis=1), jnp.concatenate(odd, axis=1)
    evens[...] = dot(even, table[0][...]) + dot(even, table[1][...])
    odds[...] = dot(odd, table[2][...]) + dot(odd, table[3][...])


def panel_blocks(rows, half):
    blocks = []
    for k in range(8):
        wanted = rows[k].reshape(8, 64, 128)[:, 32 * half : 32 * half + 32]
        blocks.append(wanted.reshape(256, 128))
    return blocks


def panel_store(out, step, lane_group, part):
    at = pl.ds(pl.multiple_of(step % 2 * 16, 16), 16)
    out[step // 2, at, 128 * lane_group : 128 * lane_group + 128] = part


def first_white_kernel(perm, *refs):
    table, (rows, out, evens, odds) = refs[:4], refs[4:]
    transform(panel_blocks(rows, 0), perm, table, evens, odds)
    whiten_strips(0, 256, evens, odds, functools.partial(panel_store, out))


def second_white_kernel(perm, *refs):
    table, (rows, mine, out, own, evens, odds, held) = refs[:4], refs[4:]
    core, _ = place()
    parts = []
    for k, block in enumerate(panel_blocks(rows, 1)):
        parts.append(jnp.concatenate([block, mine[k].astype(F32).reshape(128, 128).astype(BF)]))
    transform(parts, perm, table, evens, odds)
    whiten_strips(0, 256, evens, odds, functools.partial(panel_store, out))

    def store(step, lane_group, part):
        held[lane_group, pl.ds(pl.multiple_of(step * 16, 16), 16)] = part.astype(F32)

    whiten_strips(256, 128, evens, odds, store)
    first = iota((8, 128), 1) == 0

    def arrange(step, carry):
        window = lax.rem(step + 8 * core, 16)
        at = pl.ds(pl.multiple_of(step * 8, 8), 8)
        for chunk in range(8):
            re = held[real_group(chunk), at] * (1.0 / 16.0)
            im = held[real_group(chunk) + 2, at] * (1.0 / 16.0)
            own[window, 3 * chunk] = re
            own[window, 3 * chunk + 1] = jnp.where(first, im, im - re) if chunk == 1 else im - re
            own[window, 3 * chunk + 2] = im + re
        return carry

    lax.fori_loop(0, 16, arrange, 0, unroll=2)


def real_group(chunk):
    lanes, pair = chunk // 2, chunk % 2
    return 8 * (lanes // 2) + lanes % 2 + 4 * pair


def white_call(kernel, count, shapes, operands, scratch=()):
    return pl.pallas_call(
        kernel,
        out_shape=shapes,
        in_specs=[VMEM] * len(operands),
        out_specs=[VMEM] * len(shapes),
        scratch_shapes=[pltpu.VMEM((count, 1024), F32), pltpu.VMEM((count, 1024), F32), *scratch],
        compiler_params=PARAMS,
        cost_estimate=cost(count * 2**23, 2**22 + count * 2**13, count * 1024),
    )(*operands)


def cross_block(tile, near, far, own, raw):
    rows = slice(16 * tile, 16 * tile + 16)
    first = iota((16, 128), 1) == 0
    for chunk in range(8):
        group = real_group(chunk)
        sums = [[None] * 3 for _ in range(16)]
        for w in range(16):
            side = near if w < 8 else far
            re = side[w % 8, rows, 128 * group : 128 * group + 128].astype(F32)
            im = side[w % 8, rows, 128 * group + 256 : 128 * group + 384].astype(F32)
            both = re + (jnp.where(first, 0.0, im) if chunk == 1 else im)
            for c in range(8):
                at = pl.ds(c, 8, stride=0)
                mine = [own[w, 3 * chunk + k, at, :] for k in range(3)]
                for t in range(2):
                    total = sums[2 * c + t]
                    for k, picked in enumerate((both, im, re)):
                        term = picked[8 * t : 8 * t + 8] * mine[k]
                        total[k] = term if total[k] is None else total[k] + term
        for index, (a, b, c) in enumerate(sums):
            if chunk == 1:
                edge = first[:8]
                results = jnp.where(edge, a, a + b), jnp.where(edge, b, c - a)
            else:
                results = a + b, c - a
            for k, part in enumerate(results):
                raw[group + 2 * k, pl.ds(index % 2 * 64 + index // 2, 8, stride=8), :] = part


def round_cross(raw, cross):
    for g in range(16):
        cross[:, 128 * g : 128 * g + 128] = raw[g].astype(BF)


def cross_tiles(near, far, own, raw, cross):
    for tile in range(2):
        cross_block(tile, near, far, own, raw)
        for g in range(16):
            cross[128 * tile : 128 * tile + 128, 128 * g : 128 * g + 128] = raw[g].astype(BF)


def lag_products(half, cross, lag_even, lag_odd, out, stage, sems):
    copies = []
    width = 1024 // PIECES
    for piece in range(PIECES):
        lower = slice(width * piece, width * piece + width)
        upper = slice(1024 + width * piece, 1024 + width * piece + width)
        evens = dot(cross[:, :1024], lag_even[:, lower])
        odds = dot(cross[:, 1024:], lag_odd[:, lower])
        stage[half, :, :, lower] = (evens - odds).reshape(32, 8, width)
        stage[half, :, :, upper] = (evens + odds).reshape(32, 8, width)
        for k, lanes in enumerate((lower, upper)):
            copy = pltpu.make_async_copy(
                stage.at[half, :, :, lanes],
                out.at[32 * half : 32 * half + 32, :, lanes],
                sems.at[half, 2 * piece + k],
            )
            copy.start()
            copies.append(copy)
    return copies


def first_cross_kernel(near, far, own, cross, raw):
    cross_tiles(near, far, own, raw, cross)


def first_cross(near, far, own):
    return pl.pallas_call(
        first_cross_kernel,
        out_shape=jax.ShapeDtypeStruct((256, 2048), BF),
        in_specs=[VMEM] * 3,
        out_specs=VMEM,
        scratch_shapes=[pltpu.VMEM((16, 128, 128), F32)],
        compiler_params=PARAMS,
        cost_estimate=cost(2**32, 9 * 2**20),
    )(near, far, own)


def last_kernel(near, far, own, lag_even, lag_odd, before, out, raw, cross, stage, sems):
    copies = lag_products(0, before, lag_even, lag_odd, out, stage, sems)
    cross_tiles(near, far, own, raw, cross)
    copies += lag_products(1, cross, lag_even, lag_odd, out, stage, sems)
    for copy in copies:
        copy.wait()


def correlate(near, far, own, lag, before):
    return pl.pallas_call(
        last_kernel,
        out_shape=jax.ShapeDtypeStruct((64, 8, 2048), F32),
        in_specs=[VMEM] * 6,
        out_specs=ANYWHERE,
        scratch_shapes=[
            pltpu.VMEM((16, 128, 128), F32),
            pltpu.VMEM((256, 2048), BF),
            pltpu.VMEM((2, 32, 8, 2048), F32),
            pltpu.SemaphoreType.DMA((2, 2 * PIECES)),
        ],
        compiler_params=PARAMS,
        cost_estimate=cost(2**33, 9 * 2**20),
    )(near, far, own, *lag, before)


def local(strain, sources):
    window_rows = lax.all_to_all(spread(strain), "chan", 0, 0, tiled=True)
    shared = share(strain, sources)
    everyone = [shared]
    for k in range(1, 8):
        turns = (k, 8 - k)
        pairs = [(8 * i + j, 8 * i + (j ^ turns[i % 2])) for i in range(32) for j in range(8)]
        everyone.append(lax.ppermute(shared, ("chan", "stack"), pairs))
    picked, blocks = pick(window_rows, everyone)
    rows = lax.all_to_all(picked, "stack", 0, 0, tiled=True)
    tables = [jnp.asarray(t) for t in (deinterleave(), *forward_tables())]
    lag = [jnp.asarray(t) for t in lag_tables()]
    panel = jax.ShapeDtypeStruct((8, 32, 2048), BF)
    mine = jax.ShapeDtypeStruct((16, 24, 8, 128), F32)
    swap = functools.partial(lax.ppermute, axis_name="chan", perm=[(i, i ^ 1) for i in range(32)])
    (near_0,) = white_call(first_white_kernel, 256, [panel], [*tables, rows])
    far_0 = swap(near_0)
    held = [pltpu.VMEM((16, 128, 128), F32)]
    near_1, own = white_call(second_white_kernel, 384, [panel, mine], [*tables, rows, blocks], held)
    far_1 = swap(near_1)
    return correlate(near_1, far_1, own, lag, first_cross(near_0, far_0, own))


def solution(mesh):
    placed = (P(None, "chan", "stack"), P(None, "stack"))
    return jax.shard_map(
        local, mesh=mesh, in_specs=placed, out_specs=P("stack", "chan", None), check_vma=False
    )
```

```python
import functools
import math

import jax
import jax.numpy as jnp
import ml_dtypes
import numpy as np
from jax import lax
from jax.experimental import pallas as pl
from jax.experimental.pallas import tpu as pltpu
from jax.sharding import PartitionSpec as P

NS = 1024
BF = jnp.bfloat16
F32 = jnp.float32
MESH_CORES = 2
PIECES = 4


def pair_order():
    return np.concatenate([np.arange(0, 512, 2), np.arange(1, 512, 2)])


def split_table(values):
    high = values.astype(ml_dtypes.bfloat16)
    low = (values - high.astype(np.float64)).astype(ml_dtypes.bfloat16)
    return high, low


@functools.lru_cache(None)
def forward_tables():
    freq = pair_order()
    tables = []
    for odd in range(2):
        times = np.arange(odd, NS, 2)[:, None]
        phase = (times * freq[None, :] % 2048) * (2.0 * math.pi / 2048)
        cosine, sine = np.cos(phase), np.sin(phase)
        middle = (times[:, 0] * 512 % 2048) * (2.0 * math.pi / 2048)
        sine[:, 0] = -np.sin(middle) if odd else np.cos(middle)
        tables += split_table(np.concatenate([cosine, sine], axis=1))
    return tuple(tables)


@functools.lru_cache(None)
def lag_tables():
    freq = pair_order()
    lags = np.arange(1024)[None, :]
    parts = []
    for side in (freq, 1024 - freq):
        phase = (side[:, None] * lags % 2048) * (2.0 * math.pi / 2048)
        parts.append([2.0 * np.cos(phase), -2.0 * np.sin(phase)])
    middle = (512 * lags[0] % 2048) * (2.0 * math.pi / 2048)
    parts[0][0][0] = 2.0 * np.cos(middle)
    parts[0][1][0] = -2.0 * np.sin(middle)
    parts[1][0][0] = 1.0
    parts[1][1][0] = np.where(lags[0] % 2, -1.0, 1.0)
    tables = []
    for half in range(2):
        rows = slice(256 * half, 256 * half + 256)
        stacked = np.concatenate([part[rows] for pair in parts for part in pair], axis=0)
        tables.append((stacked / math.sqrt(2048)).astype(ml_dtypes.bfloat16))
    return tuple(tables)


@functools.lru_cache(None)
def deinterleave():
    table = np.zeros((256, 256), ml_dtypes.bfloat16)
    time = np.arange(256)
    table[time, (time % 2) * 128 + time // 2] = 1
    return table


def dot(a, b, dims=((1,), (0,))):
    return lax.dot_general(a, b, (dims, ((), ())), preferred_element_type=F32)


def iota(shape, dim):
    return lax.broadcasted_iota(jnp.int32, shape, dim)


VMEM = pl.BlockSpec(memory_space=pltpu.VMEM)
ANYWHERE = pl.BlockSpec(memory_space=pl.ANY)
PARAMS = pltpu.CompilerParams(vmem_limit_bytes=16 * 1024 * 1024)


def place():
    return lax.axis_index("chan") % MESH_CORES, lax.axis_index("stack")


def cost(flops, moved=2**20, special=0):
    return pl.CostEstimate(flops=flops, bytes_accessed=moved, transcendentals=special)


def spread_kernel(strain, theirs, sends, sems):
    core, _ = place()
    windows = pl.ds(8 * core, 8)
    copies = []
    for other in range(16):
        for k, (side, rows) in enumerate(((core, strain), (1 - core, theirs))):
            sem = sems.at[2 * other + k]
            copies.append(pltpu.make_async_copy(rows.at[windows], sends.at[other, side], sem))
    for copy in copies:
        copy.start()
    for copy in copies:
        copy.wait()


def spread(strain, theirs):
    return pl.pallas_call(
        spread_kernel,
        out_shape=jax.ShapeDtypeStruct((16, 2, 8, 8, 128), BF),
        in_specs=[ANYWHERE, ANYWHERE],
        out_specs=ANYWHERE,
        scratch_shapes=[pltpu.SemaphoreType.DMA((32,))],
        compiler_params=PARAMS,
        cost_estimate=cost(2**32),
    )(strain, theirs)


def share_kernel(strain, sources, shared):
    _, group = place()
    picks = sources[...].astype(F32)
    both = jnp.concatenate([picks, picks], axis=1)
    both = jnp.where(iota((16, 128), 1) // 64 == group % 2, both, 0.0)
    shared[:16] = strain[...]
    shared[16:] = both.reshape(2, 8, 128).astype(BF)


def share(strain, sources):
    return pl.pallas_call(
        share_kernel,
        out_shape=jax.ShapeDtypeStruct((18, 8, 128), BF),
        in_specs=[VMEM, VMEM],
        out_specs=VMEM,
        compiler_params=PARAMS,
        cost_estimate=cost(2**28),
    )(strain, sources)


def join_kernel(first, second, out):
    out[:18] = first[...]
    out[18:] = second[...]


def join(first, second):
    return pl.pallas_call(
        join_kernel,
        out_shape=jax.ShapeDtypeStruct((36, 8, 128), BF),
        in_specs=[VMEM, VMEM],
        out_specs=VMEM,
        compiler_params=PARAMS,
        cost_estimate=cost(2**28),
    )(first, second)


def pick_kernel(window_rows, *rest):
    shared, (out, blocks, picks) = rest[:4], rest[-3:]
    core, group = place()
    for k in range(4):
        nearest = group ^ (k + core * (4 - 2 * k) if k else 0)
        for side in range(2):
            sender, held = nearest ^ (4 * side), shared[k][18 * side : 18 * side + 18]
            picks[sender] = held[16:].astype(F32).reshape(16, 128)
            blocks[sender] = held[:16]
    chosen = iota((16, 8), 0) == 8 * core + iota((16, 8), 1)
    chosen = chosen.astype(F32).astype(BF)
    columns = []
    for pair in range(4):
        both = (picks[2 * pair] + picks[2 * pair + 1]).astype(BF)
        columns.append(dot(both, chosen, ((0,), (0,))))
    column = jnp.concatenate(columns, axis=0)
    channel = iota((512, 256), 1).astype(F32)
    for w in range(8):
        hits = (column[:, w : w + 1] == channel).astype(F32).astype(BF)
        rows = window_rows[:, :, w].astype(F32).reshape(256, 128).astype(BF)
        found = dot(hits, rows).astype(BF)
        for other in range(8):
            out[other, 64 * w : 64 * w + 64] = found[64 * other : 64 * other + 64]


def pick(window_rows, shared):
    return pl.pallas_call(
        pick_kernel,
        out_shape=(
            jax.ShapeDtypeStruct((8, 512, 128), BF),
            jax.ShapeDtypeStruct((8, 16, 8, 128), BF),
        ),
        in_specs=[VMEM] * 5,
        out_specs=(VMEM, VMEM),
        scratch_shapes=[pltpu.VMEM((8, 16, 128), F32)],
        compiler_params=PARAMS,
        cost_estimate=cost(2**33),
    )(window_rows, *shared)


def whiten_strips(start, count, evens, odds, store):
    def strip(step, carry):
        at = pl.ds(pl.multiple_of(start + step * 16, 16), 16)
        first = iota((16, 128), 1) == 0
        held, total = [], None
        for k in range(4):
            near, far = slice(128 * k, 128 * k + 128), slice(512 + 128 * k, 640 + 128 * k)
            a, c, b, d = evens[at, near], evens[at, far], odds[at, near], odds[at, far]
            re_1, im_1, re_2, im_2 = a + b, c + d, a - b, c - d
            if k == 0:
                re_2, im_2 = jnp.where(first, re_1, re_2), jnp.where(first, re_2, im_2)
                re_1, im_1 = jnp.where(first, c, re_1), jnp.where(first, -d, im_1)
            power_1 = re_1 * re_1 + im_1 * im_1
            square_re, square_im = re_2 * re_2, im_2 * im_2
            power_2 = square_re + square_im
            both = power_1 + power_2
            total = both if total is None else total + both
            held.append((re_1, im_1, re_2, im_2, power_1, square_re, square_im, power_2))
        level = jnp.sum(total, axis=1, keepdims=True) * (1.0 / 1025.0)
        floor = 0.05 * level + 1e-06
        for k, (re_1, im_1, re_2, im_2, power_1, square_re, square_im, power_2) in enumerate(held):
            factor_1 = lax.rsqrt(power_1 + floor)
            if k == 0:
                factor_re = lax.rsqrt(jnp.where(first, square_re, power_2) + floor)
                factor_im = lax.rsqrt(jnp.where(first, square_im, power_2) + floor)
            else:
                factor_re = factor_im = lax.rsqrt(power_2 + floor)
            parts = (re_1 * factor_1, -im_1 * factor_1, re_2 * factor_re, im_2 * factor_im)
            for index, part in enumerate(parts):
                store(step, 8 * (k // 2) + 2 * index + k % 2, part.astype(BF))
        return carry

    lax.fori_loop(0, count // 16, strip, 0, unroll=4)


def transform(blocks, perm, table, evens, odds):
    even, odd = [], []
    for pair in range(4):
        block = jnp.concatenate(blocks[2 * pair : 2 * pair + 2], axis=1)
        apart = dot(block, perm[...]).astype(BF)
        even.append(apart[:, :128])
        odd.append(apart[:, 128:])
    even, odd = jnp.concatenate(even, axis=1), jnp.concatenate(odd, axis=1)
    evens[...] = dot(even, table[0][...]) + dot(even, table[1][...])
    odds[...] = dot(odd, table[2][...]) + dot(odd, table[3][...])


def panel_blocks(rows, half):
    blocks = []
    for k in range(8):
        wanted = rows[k].reshape(8, 64, 128)[:, 32 * half : 32 * half + 32]
        blocks.append(wanted.reshape(256, 128))
    return blocks


def panel_store(out, step, lane_group, part):
    at = pl.ds(pl.multiple_of(step % 2 * 16, 16), 16)
    out[step // 2, at, 128 * lane_group : 128 * lane_group + 128] = part


def first_white_kernel(perm, *refs):
    table, (rows, out, evens, odds) = refs[:4], refs[4:]
    transform(panel_blocks(rows, 0), perm, table, evens, odds)
    whiten_strips(0, 256, evens, odds, functools.partial(panel_store, out))


def second_white_kernel(perm, *refs):
    table, (rows, mine, out, own, evens, odds, held) = refs[:4], refs[4:]
    core, _ = place()
    parts = []
    for k, block in enumerate(panel_blocks(rows, 1)):
        parts.append(jnp.concatenate([block, mine[k].astype(F32).reshape(128, 128).astype(BF)]))
    transform(parts, perm, table, evens, odds)
    whiten_strips(0, 256, evens, odds, functools.partial(panel_store, out))

    def store(step, lane_group, part):
        held[lane_group, pl.ds(pl.multiple_of(step * 16, 16), 16)] = part.astype(F32)

    whiten_strips(256, 128, evens, odds, store)
    first = iota((8, 128), 1) == 0

    def arrange(step, carry):
        window = lax.rem(step + 8 * core, 16)
        at = pl.ds(pl.multiple_of(step * 8, 8), 8)
        for chunk in range(8):
            re = held[real_group(chunk), at] * (1.0 / 16.0)
            im = held[real_group(chunk) + 2, at] * (1.0 / 16.0)
            own[window, 3 * chunk] = re
            own[window, 3 * chunk + 1] = jnp.where(first, im, im - re) if chunk == 1 else im - re
            own[window, 3 * chunk + 2] = im + re
        return carry

    lax.fori_loop(0, 16, arrange, 0, unroll=2)


def real_group(chunk):
    lanes, pair = chunk // 2, chunk % 2
    return 8 * (lanes // 2) + lanes % 2 + 4 * pair


def white_call(kernel, count, shapes, operands, scratch=()):
    return pl.pallas_call(
        kernel,
        out_shape=shapes,
        in_specs=[VMEM] * len(operands),
        out_specs=[VMEM] * len(shapes),
        scratch_shapes=[pltpu.VMEM((count, 1024), F32), pltpu.VMEM((count, 1024), F32), *scratch],
        compiler_params=PARAMS,
        cost_estimate=cost(count * 2**23, 2**22 + count * 2**13, count * 1024),
    )(*operands)


def cross_block(tile, near, far, own, raw):
    rows = slice(16 * tile, 16 * tile + 16)
    first = iota((16, 128), 1) == 0
    for chunk in range(8):
        group = real_group(chunk)
        sums = [[None] * 3 for _ in range(16)]
        for w in range(16):
            side = near if w < 8 else far
            re = side[w % 8, rows, 128 * group : 128 * group + 128].astype(F32)
            im = side[w % 8, rows, 128 * group + 256 : 128 * group + 384].astype(F32)
            both = re + (jnp.where(first, 0.0, im) if chunk == 1 else im)
            for c in range(8):
                at = pl.ds(c, 8, stride=0)
                mine = [own[w, 3 * chunk + k, at, :] for k in range(3)]
                for t in range(2):
                    total = sums[2 * c + t]
                    for k, picked in enumerate((both, im, re)):
                        term = picked[8 * t : 8 * t + 8] * mine[k]
                        total[k] = term if total[k] is None else total[k] + term
        for index, (a, b, c) in enumerate(sums):
            if chunk == 1:
                edge = first[:8]
                results = jnp.where(edge, a, a + b), jnp.where(edge, b, c - a)
            else:
                results = a + b, c - a
            for k, part in enumerate(results):
                raw[group + 2 * k, pl.ds(index % 2 * 64 + index // 2, 8, stride=8), :] = part


def round_cross(raw, cross):
    for g in range(16):
        cross[:, 128 * g : 128 * g + 128] = raw[g].astype(BF)


def cross_tiles(near, far, own, raw, cross):
    for tile in range(2):
        cross_block(tile, near, far, own, raw)
        for g in range(16):
            cross[128 * tile : 128 * tile + 128, 128 * g : 128 * g + 128] = raw[g].astype(BF)


def lag_products(half, cross, lag_even, lag_odd, out, stage, sems):
    copies = []
    width = 1024 // PIECES
    for piece in range(PIECES):
        lower = slice(width * piece, width * piece + width)
        upper = slice(1024 + width * piece, 1024 + width * piece + width)
        evens = dot(cross[:, :1024], lag_even[:, lower])
        odds = dot(cross[:, 1024:], lag_odd[:, lower])
        stage[half, :, :, lower] = (evens - odds).reshape(32, 8, width)
        stage[half, :, :, upper] = (evens + odds).reshape(32, 8, width)
        for k, lanes in enumerate((lower, upper)):
            copy = pltpu.make_async_copy(
                stage.at[half, :, :, lanes],
                out.at[32 * half : 32 * half + 32, :, lanes],
                sems.at[half, 2 * piece + k],
            )
            copy.start()
            copies.append(copy)
    return copies


def first_cross_kernel(near, far, own, cross, raw):
    cross_tiles(near, far, own, raw, cross)


def first_cross(near, far, own):
    return pl.pallas_call(
        first_cross_kernel,
        out_shape=jax.ShapeDtypeStruct((256, 2048), BF),
        in_specs=[VMEM] * 3,
        out_specs=VMEM,
        scratch_shapes=[pltpu.VMEM((16, 128, 128), F32)],
        compiler_params=PARAMS,
        cost_estimate=cost(2**32, 9 * 2**20),
    )(near, far, own)


def last_kernel(near, far, own, lag_even, lag_odd, before, out, raw, cross, stage, sems):
    copies = lag_products(0, before, lag_even, lag_odd, out, stage, sems)
    cross_tiles(near, far, own, raw, cross)
    copies += lag_products(1, cross, lag_even, lag_odd, out, stage, sems)
    for copy in copies:
        copy.wait()


def correlate(near, far, own, lag, before):
    return pl.pallas_call(
        last_kernel,
        out_shape=jax.ShapeDtypeStruct((64, 8, 2048), F32),
        in_specs=[VMEM] * 6,
        out_specs=ANYWHERE,
        scratch_shapes=[
            pltpu.VMEM((16, 128, 128), F32),
            pltpu.VMEM((256, 2048), BF),
            pltpu.VMEM((2, 32, 8, 2048), F32),
            pltpu.SemaphoreType.DMA((2, 2 * PIECES)),
        ],
        compiler_params=PARAMS,
        cost_estimate=cost(2**33, 9 * 2**20),
    )(near, far, own, *lag, before)


def local(strain, sources):
    swap = functools.partial(lax.ppermute, axis_name="chan", perm=[(i, i ^ 1) for i in range(32)])
    groups = [list(range(core, 32, 2)) for core in range(MESH_CORES)]
    window_rows = lax.all_to_all(
        spread(strain, swap(strain)), "chan", 0, 0, tiled=True, axis_index_groups=groups
    )
    shared = share(strain, sources)
    shared = join(shared, lax.ppermute(shared, "stack", [(j, j ^ 4) for j in range(8)]))
    everyone = [shared]
    for k in range(1, 4):
        turns = (k, 4 - k)
        pairs = [(8 * i + j, 8 * i + (j ^ turns[i % 2])) for i in range(32) for j in range(8)]
        everyone.append(lax.ppermute(shared, ("chan", "stack"), pairs))
    picked, blocks = pick(window_rows, everyone)
    rows = lax.all_to_all(picked, "stack", 0, 0, tiled=True)
    tables = [jnp.asarray(t) for t in (deinterleave(), *forward_tables())]
    lag = [jnp.asarray(t) for t in lag_tables()]
    panel = jax.ShapeDtypeStruct((8, 32, 2048), BF)
    mine = jax.ShapeDtypeStruct((16, 24, 8, 128), F32)
    (near_0,) = white_call(first_white_kernel, 256, [panel], [*tables, rows])
    far_0 = swap(near_0)
    held = [pltpu.VMEM((16, 128, 128), F32)]
    near_1, own = white_call(second_white_kernel, 384, [panel, mine], [*tables, rows, blocks], held)
    far_1 = swap(near_1)
    return correlate(near_1, far_1, own, lag, first_cross(near_0, far_0, own))


def solution(mesh):
    placed = (P(None, "chan", "stack"), P(None, "stack"))
    return jax.shard_map(
        local, mesh=mesh, in_specs=placed, out_specs=P("stack", "chan", None), check_vma=False
    )
```

```python
import functools
import math

import jax
import jax.numpy as jnp
import ml_dtypes
import numpy as np
from jax import lax
from jax.experimental import pallas as pl
from jax.experimental.pallas import tpu as pltpu
from jax.sharding import PartitionSpec as P

NS = 1024
BF = jnp.bfloat16
F32 = jnp.float32
MESH_CORES = 2
PIECES = 4


def pair_order():
    return np.concatenate([np.arange(0, 512, 2), np.arange(1, 512, 2)])


def split_table(values):
    high = values.astype(ml_dtypes.bfloat16)
    low = (values - high.astype(np.float64)).astype(ml_dtypes.bfloat16)
    return high, low


@functools.lru_cache(None)
def forward_tables():
    freq = pair_order()
    tables = []
    for odd in range(2):
        times = np.arange(odd, NS, 2)[:, None]
        phase = (times * freq[None, :] % 2048) * (2.0 * math.pi / 2048)
        cosine, sine = np.cos(phase), np.sin(phase)
        middle = (times[:, 0] * 512 % 2048) * (2.0 * math.pi / 2048)
        sine[:, 0] = -np.sin(middle) if odd else np.cos(middle)
        tables += split_table(np.concatenate([cosine, sine], axis=1))
    return tuple(tables)


@functools.lru_cache(None)
def lag_tables():
    freq = pair_order()
    lags = np.arange(1024)[None, :]
    parts = []
    for side in (freq, 1024 - freq):
        phase = (side[:, None] * lags % 2048) * (2.0 * math.pi / 2048)
        parts.append([2.0 * np.cos(phase), -2.0 * np.sin(phase)])
    middle = (512 * lags[0] % 2048) * (2.0 * math.pi / 2048)
    parts[0][0][0] = 2.0 * np.cos(middle)
    parts[0][1][0] = -2.0 * np.sin(middle)
    parts[1][0][0] = 1.0
    parts[1][1][0] = np.where(lags[0] % 2, -1.0, 1.0)
    tables = []
    for half in range(2):
        rows = slice(256 * half, 256 * half + 256)
        stacked = np.concatenate([part[rows] for pair in parts for part in pair], axis=0)
        tables.append((stacked / math.sqrt(2048)).astype(ml_dtypes.bfloat16))
    return tuple(tables)


@functools.lru_cache(None)
def deinterleave():
    table = np.zeros((256, 256), ml_dtypes.bfloat16)
    time = np.arange(256)
    table[time, (time % 2) * 128 + time // 2] = 1
    return table


def dot(a, b, dims=((1,), (0,))):
    return lax.dot_general(a, b, (dims, ((), ())), preferred_element_type=F32)


def iota(shape, dim):
    return lax.broadcasted_iota(jnp.int32, shape, dim)


VMEM = pl.BlockSpec(memory_space=pltpu.VMEM)
ANYWHERE = pl.BlockSpec(memory_space=pl.ANY)
PARAMS = pltpu.CompilerParams(vmem_limit_bytes=16 * 1024 * 1024)


def place():
    return lax.axis_index("chan") % MESH_CORES, lax.axis_index("stack")


def cost(flops, moved=2**20, special=0):
    return pl.CostEstimate(flops=flops, bytes_accessed=moved, transcendentals=special)


def spread_kernel(strain, theirs, sends, sems):
    core, _ = place()
    windows = pl.ds(8 * core, 8)
    copies = []
    for other in range(16):
        for k, (side, rows) in enumerate(((core, strain), (1 - core, theirs))):
            sem = sems.at[2 * other + k]
            copies.append(pltpu.make_async_copy(rows.at[windows], sends.at[other, side], sem))
    for copy in copies:
        copy.start()
    for copy in copies:
        copy.wait()


def spread(strain, theirs):
    return pl.pallas_call(
        spread_kernel,
        out_shape=jax.ShapeDtypeStruct((16, 2, 8, 8, 128), BF),
        in_specs=[ANYWHERE, ANYWHERE],
        out_specs=ANYWHERE,
        scratch_shapes=[pltpu.SemaphoreType.DMA((32,))],
        compiler_params=PARAMS,
        cost_estimate=cost(2**32),
    )(strain, theirs)


def share_kernel(strain, sources, shared):
    _, group = place()
    picks = sources[...].astype(F32)
    both = jnp.concatenate([picks, picks], axis=1)
    both = jnp.where(iota((16, 128), 1) // 64 == group % 2, both, 0.0)
    shared[:16] = strain[...]
    shared[16:] = both.reshape(2, 8, 128).astype(BF)


def share(strain, sources):
    return pl.pallas_call(
        share_kernel,
        out_shape=jax.ShapeDtypeStruct((18, 8, 128), BF),
        in_specs=[VMEM, VMEM],
        out_specs=VMEM,
        compiler_params=PARAMS,
        cost_estimate=cost(2**28),
    )(strain, sources)


def join_kernel(first, second, out):
    out[:18] = first[...]
    out[18:] = second[...]


def join(first, second):
    return pl.pallas_call(
        join_kernel,
        out_shape=jax.ShapeDtypeStruct((36, 8, 128), BF),
        in_specs=[VMEM, VMEM],
        out_specs=VMEM,
        compiler_params=PARAMS,
        cost_estimate=cost(2**28),
    )(first, second)


def pick_kernel(window_rows, *rest):
    shared, (out, blocks, picks) = rest[:4], rest[-3:]
    core, group = place()
    for k in range(4):
        nearest = group ^ (k + core * (4 - 2 * k) if k else 0)
        for side in range(2):
            sender, held = nearest ^ (4 * side), shared[k][18 * side : 18 * side + 18]
            picks[sender] = held[16:].astype(F32).reshape(16, 128)
            blocks[sender] = held[:16]
    chosen = iota((16, 8), 0) == 8 * core + iota((16, 8), 1)
    chosen = chosen.astype(F32).astype(BF)
    columns = []
    for pair in range(4):
        both = (picks[2 * pair] + picks[2 * pair + 1]).astype(BF)
        columns.append(dot(both, chosen, ((0,), (0,))))
    column = jnp.concatenate(columns, axis=0)
    channel = iota((512, 256), 1).astype(F32)
    for w in range(8):
        hits = (column[:, w : w + 1] == channel).astype(F32).astype(BF)
        rows = window_rows[:, :, w].astype(F32).reshape(256, 128).astype(BF)
        found = dot(hits, rows).astype(BF)
        for other in range(8):
            out[other, 64 * w : 64 * w + 64] = found[64 * other : 64 * other + 64]


def pick(window_rows, shared):
    return pl.pallas_call(
        pick_kernel,
        out_shape=(
            jax.ShapeDtypeStruct((8, 512, 128), BF),
            jax.ShapeDtypeStruct((8, 16, 8, 128), BF),
        ),
        in_specs=[VMEM] * 5,
        out_specs=(VMEM, VMEM),
        scratch_shapes=[pltpu.VMEM((8, 16, 128), F32)],
        compiler_params=PARAMS,
        cost_estimate=cost(2**33),
    )(window_rows, *shared)


def whiten_strips(start, count, evens, odds, store):
    def strip(step, carry):
        at = pl.ds(pl.multiple_of(start + step * 16, 16), 16)
        first = iota((16, 128), 1) == 0
        held, total = [], None
        for k in range(4):
            near, far = slice(128 * k, 128 * k + 128), slice(512 + 128 * k, 640 + 128 * k)
            a, c, b, d = evens[at, near], evens[at, far], odds[at, near], odds[at, far]
            re_1, im_1, re_2, im_2 = a + b, c + d, a - b, c - d
            if k == 0:
                re_2, im_2 = jnp.where(first, re_1, re_2), jnp.where(first, re_2, im_2)
                re_1, im_1 = jnp.where(first, c, re_1), jnp.where(first, -d, im_1)
            power_1 = re_1 * re_1 + im_1 * im_1
            square_re, square_im = re_2 * re_2, im_2 * im_2
            power_2 = square_re + square_im
            both = power_1 + power_2
            total = both if total is None else total + both
            held.append((re_1, im_1, re_2, im_2, power_1, square_re, square_im, power_2))
        level = jnp.sum(total, axis=1, keepdims=True) * (1.0 / 1025.0)
        floor = 0.05 * level + 1e-06
        for k, (re_1, im_1, re_2, im_2, power_1, square_re, square_im, power_2) in enumerate(held):
            factor_1 = lax.rsqrt(power_1 + floor)
            if k == 0:
                factor_re = lax.rsqrt(jnp.where(first, square_re, power_2) + floor)
                factor_im = lax.rsqrt(jnp.where(first, square_im, power_2) + floor)
            else:
                factor_re = factor_im = lax.rsqrt(power_2 + floor)
            parts = (re_1 * factor_1, -im_1 * factor_1, re_2 * factor_re, im_2 * factor_im)
            for index, part in enumerate(parts):
                store(step, 8 * (k // 2) + 2 * index + k % 2, part.astype(BF))
        return carry

    lax.fori_loop(0, count // 16, strip, 0, unroll=4)


def transform(blocks, perm, table, evens, odds):
    even, odd = [], []
    for pair in range(4):
        block = jnp.concatenate(blocks[2 * pair : 2 * pair + 2], axis=1)
        apart = dot(block, perm[...]).astype(BF)
        even.append(apart[:, :128])
        odd.append(apart[:, 128:])
    even, odd = jnp.concatenate(even, axis=1), jnp.concatenate(odd, axis=1)
    evens[...] = dot(even, table[0][...]) + dot(even, table[1][...])
    odds[...] = dot(odd, table[2][...]) + dot(odd, table[3][...])


def panel_blocks(rows, half):
    blocks = []
    for k in range(8):
        wanted = rows[k].reshape(8, 64, 128)[:, 32 * half : 32 * half + 32]
        blocks.append(wanted.reshape(256, 128))
    return blocks


def panel_store(out, step, lane_group, part):
    at = pl.ds(pl.multiple_of(step % 2 * 16, 16), 16)
    out[step // 2, at, 128 * lane_group : 128 * lane_group + 128] = part


def first_white_kernel(perm, *refs):
    table, (rows, out, evens, odds) = refs[:4], refs[4:]
    transform(panel_blocks(rows, 0), perm, table, evens, odds)
    whiten_strips(0, 256, evens, odds, functools.partial(panel_store, out))


def second_white_kernel(perm, *refs):
    table, (rows, mine, out, own, evens, odds, held) = refs[:4], refs[4:]
    core, _ = place()
    parts = []
    for k, block in enumerate(panel_blocks(rows, 1)):
        parts.append(jnp.concatenate([block, mine[k].astype(F32).reshape(128, 128).astype(BF)]))
    transform(parts, perm, table, evens, odds)
    whiten_strips(0, 256, evens, odds, functools.partial(panel_store, out))

    def store(step, lane_group, part):
        held[lane_group, pl.ds(pl.multiple_of(step * 16, 16), 16)] = part.astype(F32)

    whiten_strips(256, 128, evens, odds, store)
    first = iota((8, 128), 1) == 0

    def arrange(step, carry):
        window = lax.rem(step + 8 * core, 16)
        at = pl.ds(pl.multiple_of(step * 8, 8), 8)
        for chunk in range(8):
            re = held[real_group(chunk), at] * (1.0 / 16.0)
            im = held[real_group(chunk) + 2, at] * (1.0 / 16.0)
            own[window, 3 * chunk, :8] = re
            less = jnp.where(first, im, im - re) if chunk == 1 else im - re
            own[window, 3 * chunk + 1, :8] = less
            own[window, 3 * chunk + 2, :8] = im + re
        return carry

    lax.fori_loop(0, 16, arrange, 0, unroll=2)


def real_group(chunk):
    lanes, pair = chunk // 2, chunk % 2
    return 8 * (lanes // 2) + lanes % 2 + 4 * pair


def white_call(kernel, count, shapes, operands, scratch=()):
    return pl.pallas_call(
        kernel,
        out_shape=shapes,
        in_specs=[VMEM] * len(operands),
        out_specs=[VMEM] * len(shapes),
        scratch_shapes=[pltpu.VMEM((count, 1024), F32), pltpu.VMEM((count, 1024), F32), *scratch],
        compiler_params=PARAMS,
        cost_estimate=cost(count * 2**23, 2**22 + count * 2**13, count * 1024),
    )(*operands)


def cross_block(tile, near, far, own, raw):
    rows = slice(16 * tile, 16 * tile + 16)
    first = iota((16, 128), 1) == 0
    for chunk in range(8):
        group = real_group(chunk)
        sums = [[None] * 3 for _ in range(16)]
        for w in range(16):
            side = near if w < 8 else far
            re = side[w % 8, rows, 128 * group : 128 * group + 128].astype(F32)
            im = side[w % 8, rows, 128 * group + 256 : 128 * group + 384].astype(F32)
            both = re + (jnp.where(first, 0.0, im) if chunk == 1 else im)
            for c in range(8):
                at = pl.ds(c, 8, stride=0)
                mine = [own[w, 3 * chunk + k, at, :] for k in range(3)]
                for t in range(2):
                    total = sums[2 * c + t]
                    for k, picked in enumerate((both, im, re)):
                        term = picked[8 * t : 8 * t + 8] * mine[k]
                        total[k] = term if total[k] is None else total[k] + term
        for index, (a, b, c) in enumerate(sums):
            if chunk == 1:
                edge = first[:8]
                results = jnp.where(edge, a, a + b), jnp.where(edge, b, c - a)
            else:
                results = a + b, c - a
            for k, part in enumerate(results):
                raw[group + 2 * k, pl.ds(index % 2 * 64 + index // 2, 8, stride=8), :] = part


def round_cross(raw, cross):
    for g in range(16):
        cross[:, 128 * g : 128 * g + 128] = raw[g, :128].astype(BF)


def cross_tiles(near, far, own, raw, cross):
    for tile in range(2):
        cross_block(tile, near, far, own, raw)
        for g in range(16):
            cross[128 * tile : 128 * tile + 128, 128 * g : 128 * g + 128] = raw[g, :128].astype(BF)


def lag_products(half, cross, lag_even, lag_odd, out, stage, sems):
    copies = []
    width = 1024 // PIECES
    for piece in range(PIECES):
        lower = slice(width * piece, width * piece + width)
        upper = slice(1024 + width * piece, 1024 + width * piece + width)
        evens = dot(cross[:, :1024], lag_even[:, lower])
        odds = dot(cross[:, 1024:], lag_odd[:, lower])
        stage[half, :, :, lower] = (evens - odds).reshape(32, 8, width)
        stage[half, :, :, upper] = (evens + odds).reshape(32, 8, width)
        for k, lanes in enumerate((lower, upper)):
            copy = pltpu.make_async_copy(
                stage.at[half, :, :, lanes],
                out.at[32 * half : 32 * half + 32, :, lanes],
                sems.at[half, 2 * piece + k],
            )
            copy.start()
            copies.append(copy)
    return copies


def first_cross_kernel(near, far, own, cross, raw):
    cross_tiles(near, far, own, raw, cross)


def first_cross(near, far, own):
    return pl.pallas_call(
        first_cross_kernel,
        out_shape=jax.ShapeDtypeStruct((256, 2048), BF),
        in_specs=[VMEM] * 3,
        out_specs=VMEM,
        scratch_shapes=[pltpu.VMEM((16, 136, 128), F32)],
        compiler_params=PARAMS,
        cost_estimate=cost(2**32, 9 * 2**20),
    )(near, far, own)


def last_kernel(near, far, own, lag_even, lag_odd, before, out, raw, cross, stage, sems):
    copies = lag_products(0, before, lag_even, lag_odd, out, stage, sems)
    cross_tiles(near, far, own, raw, cross)
    copies += lag_products(1, cross, lag_even, lag_odd, out, stage, sems)
    for copy in copies:
        copy.wait()


def correlate(near, far, own, lag, before):
    return pl.pallas_call(
        last_kernel,
        out_shape=jax.ShapeDtypeStruct((64, 8, 2048), F32),
        in_specs=[VMEM] * 6,
        out_specs=ANYWHERE,
        scratch_shapes=[
            pltpu.VMEM((16, 136, 128), F32),
            pltpu.VMEM((256, 2048), BF),
            pltpu.VMEM((2, 32, 8, 2048), F32),
            pltpu.SemaphoreType.DMA((2, 2 * PIECES)),
        ],
        compiler_params=PARAMS,
        cost_estimate=cost(2**33, 9 * 2**20),
    )(near, far, own, *lag, before)


def local(strain, sources):
    swap = functools.partial(lax.ppermute, axis_name="chan", perm=[(i, i ^ 1) for i in range(32)])
    groups = [list(range(core, 32, 2)) for core in range(MESH_CORES)]
    window_rows = lax.all_to_all(
        spread(strain, swap(strain)), "chan", 0, 0, tiled=True, axis_index_groups=groups
    )
    shared = share(strain, sources)
    shared = join(shared, lax.ppermute(shared, "stack", [(j, j ^ 4) for j in range(8)]))
    everyone = [shared]
    for k in range(1, 4):
        turns = (k, 4 - k)
        pairs = [(8 * i + j, 8 * i + (j ^ turns[i % 2])) for i in range(32) for j in range(8)]
        everyone.append(lax.ppermute(shared, ("chan", "stack"), pairs))
    picked, blocks = pick(window_rows, everyone)
    rows = lax.all_to_all(picked, "stack", 0, 0, tiled=True)
    tables = [jnp.asarray(t) for t in (deinterleave(), *forward_tables())]
    lag = [jnp.asarray(t) for t in lag_tables()]
    panel = jax.ShapeDtypeStruct((8, 32, 2048), BF)
    mine = jax.ShapeDtypeStruct((16, 24, 16, 128), F32)
    (near_0,) = white_call(first_white_kernel, 256, [panel], [*tables, rows])
    far_0 = swap(near_0)
    held = [pltpu.VMEM((16, 128, 128), F32)]
    near_1, own = white_call(second_white_kernel, 384, [panel, mine], [*tables, rows, blocks], held)
    far_1 = swap(near_1)
    return correlate(near_1, far_1, own, lag, first_cross(near_0, far_0, own))


def solution(mesh):
    placed = (P(None, "chan", "stack"), P(None, "stack"))
    return jax.shard_map(
        local, mesh=mesh, in_specs=placed, out_specs=P("stack", "chan", None), check_vma=False
    )
```
